32 devices in a mesh: rows: 16 (over z, y, x), cols: 2 (over core).
Axes of the slice: x: 2, y: 2, z: 4, core: 2. Of those that a mesh axis runs over, the one named last changes fastest.
Arguments:
- block_vector: float32 [131072, 128], P('rows'), may hold values from -6 to 6
- op_tiles: float32 [1024, 8, 128, 128], P('rows', 'cols')
- tile_cols: int32 [1024, 8], P('rows', 'cols'), may hold values from 0 to 1023, as said below
- live_counts: int32 [1024], P('rows'), may hold values from 1 to 8
Outputs:
- basis_block: float32 [131072, 128], P(('rows', 'cols'))
- r_factor: float32 [128, 128], replicated
The draws below stay inside these ranges and needn't reach their ends.
Inputs may be any that keep to these rules, and one draw needn't show every extreme that they name: `tile_cols`: slot 0 of row block i names i itself. Every entry names a row block of the same index of rows as i, or of the index just before or after it.
All inputs are finite; a program needn't handle non-finite values.
Results may differ from the reference program's by a relative error of at most 0.0003.
Values sent between devices are 32-bit elements; how exact they have to be, the bound alone decides.
A program may use at most 128 MiB of HBM per device.

```python
import jax
import jax.numpy as jnp
from jax import lax

RB_DEV = 64
TILE = 128
BW = 128
K = 8
NB = 1024
NODES = 131072


def draw_op_tiles(key, part):
    key = jax.random.fold_in(key, 11)
    key_off, key_diag = jax.random.split(key)
    off_part = jax.random.normal(key_off, (NB, K, TILE, TILE), jnp.float32) * 0.08
    top_log = jnp.log(10.0)
    uniform_draw = jax.random.uniform(key_diag, (NB, TILE), jnp.float32)
    rising = 1.0 + 2.0 * jnp.arange(NB, dtype=jnp.float32) / NB
    diag_vals = jnp.exp(uniform_draw * top_log) * rising[:, None]
    diag_tiles = diag_vals[:, :, None] * jnp.eye(TILE, dtype=jnp.float32)[None, :, :]
    return off_part.at[:, 0].add(diag_tiles)


def draw_tile_cols(key, part):
    key = jax.random.fold_in(key, 7)
    row_ids = jnp.arange(NB, dtype=jnp.int32)
    owner = row_ids // RB_DEV
    offsets = jax.random.randint(key, (NB, K), 0, 3 * RB_DEV, dtype=jnp.int32)
    targets = jnp.clip(owner[:, None] * RB_DEV - RB_DEV + offsets, 0, NB - 1)
    return targets.at[:, 0].set(row_ids).astype(jnp.int32)


def draw_live_counts(key, part):
    key = jax.random.fold_in(key, 5)
    counts_drawn = jax.random.randint(key, (NB,), 1, K + 1, dtype=jnp.int32)
    return counts_drawn.at[0].set(K).at[NB - 1].set(1).astype(jnp.int32)


def block_levels(rng, shape, shards, least, largest):
    factor_of = 1.0
    for axis_at, parts in shards:
        steps = jax.random.uniform(jax.random.fold_in(jax.random.fold_in(rng, 6), axis_at), (parts,), jnp.float32, least / len(shards), largest / len(shards))
        factor_of = factor_of * jnp.repeat(jnp.exp(steps), shape[axis_at] // parts).reshape((-1,) + (1,) * (len(shape) - 1 - axis_at))
    return factor_of


def bell_draw(own_key, dims, scale, limit, shards=(), kind=jnp.bfloat16):
    array = jax.random.normal(own_key, dims, jnp.float32) * scale
    if len(shards) > 0:
        array = block_levels(own_key, dims, shards, -0.22, 0.18) * array
    return jnp.clip(array, min=-limit, max=limit).astype(kind)


def setup_inputs(seed: int = 0) -> dict:
    keys = jax.random.split(jax.random.key(seed), 5)
    return {
        "block_vector": bell_draw(keys[0], (NODES, BW), 1.0, 6.0, ((0, 16),), jnp.float32),
        "op_tiles": draw_op_tiles(jax.random.fold_in(keys[4], 71), 0),
        "tile_cols": draw_tile_cols(jax.random.fold_in(keys[4], 71), 0),
        "live_counts": draw_live_counts(jax.random.fold_in(keys[4], 71), 0),
    }


def reference(block_vector, op_tiles, tile_cols, live_counts):
    vec_blocks = block_vector.reshape(NB, TILE, BW)
    slot_ids = jnp.arange(K, dtype=jnp.int32)

    def row_block(items):
        tiles_row, cols_row, count_row = items
        live_mask = (slot_ids < count_row).astype(jnp.float32)
        picked = vec_blocks[cols_row] * live_mask[:, None, None]
        return jnp.einsum('sab,sbc->ac', tiles_row, picked, precision=lax.Precision.HIGHEST)
    product = lax.map(row_block, (op_tiles, tile_cols, live_counts)).reshape(NODES, BW)
    gram_matrix = jnp.einsum('ra,rb->ab', product, product, precision=lax.Precision.HIGHEST)
    chol_lower = jnp.linalg.cholesky(gram_matrix)
    solved = jax.scipy.linalg.solve_triangular(chol_lower, product.T, lower=True)
    root_nodes = jnp.sqrt(jnp.float32(NODES))
    return (solved.T * root_nodes, chol_lower.T / root_nodes)
```

```python
import functools
import math

import jax
import jax.numpy as jnp
from jax import lax
from jax.experimental import pallas as pl
from jax.experimental.pallas import tpu as pltpu
from jax.sharding import PartitionSpec as P

MESH = pl.DeviceIdType.MESH
BF16 = jnp.bfloat16
F32 = jnp.float32
MIB = 1024 * 1024
PANEL = 16


def split2(x):
    hi = x.astype(BF16)
    lo = (x - hi.astype(F32)).astype(BF16)
    return hi, lo


def greet(peers):
    barrier = pltpu.get_barrier_semaphore()
    for cond, device in peers:
        if cond is None:
            pl.semaphore_signal(barrier, inc=1, device_id=device, device_id_type=MESH)
        else:
            @pl.when(cond)
            def _(device=device):
                pl.semaphore_signal(barrier, inc=1, device_id=device, device_id_type=MESH)
    total = 0
    for cond, _ in peers:
        total = total + (1 if cond is None else jnp.where(cond, 1, 0))
    pl.semaphore_wait(barrier, total)


def relay_kernel(n_rows, n_cols, chunks, ahead, own, halo, near_s, near_r, far_s, far_r, sib_s, sib_r):
    r = lax.axis_index("rows")
    c = lax.axis_index("cols")
    odd = lax.rem(r, 2)
    partner = r + 1 - 2 * odd
    fwd_to = r + 2 - 4 * odd
    far_from = r - 2 + 4 * odd
    can_fwd = (fwd_to >= 0) & (fwd_to < n_rows)
    has_far = (far_from >= 0) & (far_from < n_rows)
    part = own.shape[0] // n_cols
    size = part // chunks
    near_slot = 1 - odd
    far_slot = odd

    peers = [(None, (partner, c)), (can_fwd, (fwd_to, c)), (has_far, (far_from, c))]
    peers += [(None, (r, lax.rem(c + d, n_cols))) for d in range(1, n_cols)]
    greet(peers)

    def rows_of(i, col):
        return pl.ds(pl.multiple_of(col * part + i * size, size), size)

    def near(i):
        return pltpu.make_async_remote_copy(
            src_ref=own.at[rows_of(i, c)], dst_ref=halo.at[odd, rows_of(i, c)],
            send_sem=near_s.at[i], recv_sem=near_r.at[i], device_id=(partner, c), device_id_type=MESH)

    def near_in(i):
        return pltpu.make_async_remote_copy(
            src_ref=own.at[rows_of(i, c)], dst_ref=halo.at[near_slot, rows_of(i, c)],
            send_sem=near_s.at[i], recv_sem=near_r.at[i], device_id=(partner, c), device_id_type=MESH)

    def far(i):
        return pltpu.make_async_remote_copy(
            src_ref=halo.at[near_slot, rows_of(i, c)], dst_ref=halo.at[far_slot, rows_of(i, c)],
            send_sem=far_s.at[i], recv_sem=far_r.at[i], device_id=(fwd_to, c), device_id_type=MESH)

    def sib(i, kind, d):
        slot = near_slot if kind == 0 else far_slot
        k = (kind * (n_cols - 1) + d - 1) * chunks + i
        return pltpu.make_async_remote_copy(
            src_ref=halo.at[slot, rows_of(i, c)], dst_ref=halo.at[slot, rows_of(i, c)],
            send_sem=sib_s.at[k], recv_sem=sib_r.at[k],
            device_id=(r, lax.rem(c + d, n_cols)), device_id_type=MESH)

    def sib_in(i, kind, d):
        slot = near_slot if kind == 0 else far_slot
        k = (kind * (n_cols - 1) + d - 1) * chunks + i
        col = lax.rem(c + n_cols - d, n_cols)
        return pltpu.make_async_remote_copy(
            src_ref=halo.at[slot, rows_of(i, c)], dst_ref=halo.at[slot, rows_of(i, col)],
            send_sem=sib_s.at[k], recv_sem=sib_r.at[k],
            device_id=(r, lax.rem(c + d, n_cols)), device_id_type=MESH)

    for i in range(ahead):
        near(i).start()

    @pl.loop(0, chunks + 1)
    def _(i):
        @pl.when(i < chunks)
        def _():
            near_in(i).wait_recv()

            @pl.when(can_fwd)
            def _():
                far(i).start()

            for d in range(1, n_cols):
                sib(i, 0, d).start()

            @pl.when(i + ahead < chunks)
            def _():
                near(i + ahead).start()

        @pl.when((i > 0) & has_far)
        def _():
            far(i - 1).wait_recv()
            for d in range(1, n_cols):
                sib(i - 1, 1, d).start()

    @pl.loop(0, chunks)
    def _(i):
        for d in range(1, n_cols):
            sib_in(i, 0, d).wait_recv()
            sib(i, 0, d).wait_send()

        @pl.when(has_far)
        def _():
            for d in range(1, n_cols):
                sib_in(i, 1, d).wait_recv()
                sib(i, 1, d).wait_send()

        near(i).wait_send()

        @pl.when(can_fwd)
        def _():
            far(i).wait_send()


def relay(block_vector, n_rows, n_cols):
    rows, width = block_vector.shape
    chunks = 16
    dma = pltpu.SemaphoreType.DMA
    n_sib = max(1, 2 * (n_cols - 1) * chunks)
    return pl.pallas_call(
        functools.partial(relay_kernel, n_rows, n_cols, chunks, 4),
        out_shape=jax.ShapeDtypeStruct((2, rows, width), F32),
        in_specs=[pl.BlockSpec(memory_space=pl.ANY)],
        out_specs=pl.BlockSpec(memory_space=pl.ANY),
        scratch_shapes=[dma((chunks,)), dma((chunks,)), dma((chunks,)), dma((chunks,)), dma((n_sib,)), dma((n_sib,))],
        compiler_params=pltpu.CompilerParams(collective_id=0, has_side_effects=True),
        name="halo_relay",
    )(block_vector)


def product_kernel(group, place, cols, counts, own, halo, tiles, out, ext, sems):
    g = pl.program_id(0)
    rows = own.shape[0]
    slots = tiles.shape[1]
    size = tiles.shape[2]
    blocks = rows // size

    @pl.when(g == 0)
    def _():
        moves = [
            pltpu.make_async_copy(halo.at[0], ext.at[pl.ds(0, rows)], sems.at[0]),
            pltpu.make_async_copy(own, ext.at[pl.ds(rows, rows)], sems.at[1]),
            pltpu.make_async_copy(halo.at[1], ext.at[pl.ds(2 * rows, rows)], sems.at[2]),
        ]
        for m in moves:
            m.start()
        for m in moves:
            m.wait()

    first_block = (place[0] - 1) * blocks
    first_slot = place[1] * slots

    @pl.loop(0, group)
    def _(j):
        row = g * group + j
        live = counts[row] - first_slot
        where = pl.ds(pl.multiple_of(j * size, size), size)

        @pl.when(live <= 0)
        def _():
            out[where, :] = jnp.zeros((size, out.shape[1]), F32)

        @pl.when(live > 0)
        def _():
            a_parts = []
            b_parts = []
            for s in range(slots):
                at = jnp.clip(cols[row, s] - first_block, 0, 3 * blocks - 1)
                b = ext[pl.ds(pl.multiple_of(at * size, size), size), :]
                b_parts.append(jnp.where(s < live, b, 0.0))
                a_parts.append(tiles[j, s])
            a_hi, a_lo = split2(jnp.concatenate(a_parts, axis=1))
            b_hi, b_lo = split2(jnp.concatenate(b_parts, axis=0))
            both = jnp.dot(a_hi, jnp.concatenate([b_hi, b_lo], axis=1), preferred_element_type=F32)
            rest = jnp.dot(a_lo, b_hi, preferred_element_type=F32)
            width = out.shape[1]
            out[where, :] = both[:, :width] + both[:, width:] + rest


def products(place, tile_cols, live_counts, block_vector, halo, op_tiles):
    blocks, slots, size, _ = op_tiles.shape
    rows, width = block_vector.shape
    group = 4
    return pl.pallas_call(
        functools.partial(product_kernel, group),
        out_shape=jax.ShapeDtypeStruct((rows, width), F32),
        grid_spec=pltpu.PrefetchScalarGridSpec(
            num_scalar_prefetch=3,
            grid=(blocks // group,),
            in_specs=[
                pl.BlockSpec(memory_space=pl.ANY),
                pl.BlockSpec(memory_space=pl.ANY),
                pl.BlockSpec((group, slots, size, size), lambda g, *_: (g, 0, 0, 0)),
            ],
            out_specs=pl.BlockSpec((group * size, width), lambda g, *_: (g, 0)),
            scratch_shapes=[pltpu.VMEM((3 * rows, width), F32), pltpu.SemaphoreType.DMA((3,))],
        ),
        compiler_params=pltpu.CompilerParams(vmem_limit_bytes=40 * MIB),
        name="tile_products",
    )(place, tile_cols, live_counts, block_vector, halo, op_tiles)


def gram_kernel(n_rows, n_cols, chunks, partial, rows_out, gram_out, got, acc, into, part_s, part_r, sum_s, sum_r):
    r = lax.axis_index("rows")
    c = lax.axis_index("cols")
    part = partial.shape[0] // n_cols
    size = part // chunks
    steps = int(math.log2(n_rows))
    width = partial.shape[1]

    peers = [(None, (r, lax.rem(c + d, n_cols))) for d in range(1, n_cols)]
    row_peers = []
    for s in range(steps):
        bit = lax.rem(r // (1 << s), 2)
        row_peers.append(r + (1 << s) * (1 - 2 * bit))
    peers += [(None, (p, c)) for p in row_peers]
    greet(peers)

    def give(i, d):
        to = lax.rem(c + d, n_cols)
        src = pl.ds(pl.multiple_of(to * part + i * size, size), size)
        dst = pl.ds(pl.multiple_of(i * size, size), size)
        k = (d - 1) * chunks + i
        return pltpu.make_async_remote_copy(
            src_ref=partial.at[src], dst_ref=got.at[d - 1, dst], send_sem=part_s.at[k], recv_sem=part_r.at[k],
            device_id=(r, to), device_id_type=MESH)

    @pl.loop(0, chunks)
    def _(i):
        for d in range(1, n_cols):
            give(i, d).start()

    acc[0] = jnp.zeros_like(acc.at[0])

    @pl.loop(0, chunks)
    def _(i):
        here = pl.ds(pl.multiple_of(i * size, size), size)
        x = partial[pl.ds(pl.multiple_of(c * part + i * size, size), size), :]
        for d in range(1, n_cols):
            give(i, d).wait_recv()
            x = x + got[d - 1, here, :]
        rows_out[here, :] = x
        hi, lo = split2(x)
        both = jnp.concatenate([hi, lo], axis=1)
        g = lax.dot_general(both, both, (((0,), (0,)), ((), ())), preferred_element_type=F32)
        acc[0] += (g[:width, :width] + g[width:, width:]) + (g[:width, width:] + g[width:, :width])

    def add_up(s, k, device):
        return pltpu.make_async_remote_copy(
            src_ref=acc.at[s], dst_ref=into.at[k], send_sem=sum_s.at[k], recv_sem=sum_r.at[k],
            device_id=device, device_id_type=MESH)

    sent = []
    s = 0
    if n_cols == 2:
        sent.append(add_up(0, 0, (r, 1 - c)))
        sent[-1].start()
        sent[-1].wait_recv()
        acc[1] = acc[0] + into[0]
        s = 1
    elif n_cols > 2:
        bits = int(math.log2(n_cols))
        for b in range(bits):
            bit = lax.rem(c // (1 << b), 2)
            sent.append(add_up(s, s, (r, c + (1 << b) * (1 - 2 * bit))))
            sent[-1].start()
            sent[-1].wait_recv()
            acc[s + 1] = acc[s] + into[s]
            s += 1
    for p in row_peers:
        sent.append(add_up(s, s, (p, c)))
        sent[-1].start()
        sent[-1].wait_recv()
        acc[s + 1] = acc[s] + into[s]
        s += 1
    gram_out[...] = acc[s]
    for copy in sent:
        copy.wait_send()

    @pl.loop(0, chunks)
    def _(i):
        for d in range(1, n_cols):
            give(i, d).wait_send()


def rows_and_gram(partial, n_rows, n_cols):
    rows, width = partial.shape
    part = rows // n_cols
    chunks = 4
    steps = int(math.log2(n_rows * n_cols))
    n_give = max(1, (n_cols - 1) * chunks)
    dma = pltpu.SemaphoreType.DMA
    vmem = pl.BlockSpec(memory_space=pltpu.VMEM)
    return pl.pallas_call(
        functools.partial(gram_kernel, n_rows, n_cols, chunks),
        out_shape=(jax.ShapeDtypeStruct((part, width), F32), jax.ShapeDtypeStruct((width, width), F32)),
        in_specs=[vmem],
        out_specs=(vmem, vmem),
        scratch_shapes=[
            pltpu.VMEM((max(1, n_cols - 1), part, width), F32),
            pltpu.VMEM((steps + 1, width, width), F32),
            pltpu.VMEM((max(1, steps), width, width), F32),
            dma((n_give,)), dma((n_give,)), dma((max(1, steps),)), dma((max(1, steps),)),
        ],
        compiler_params=pltpu.CompilerParams(collective_id=1, has_side_effects=True, vmem_limit_bytes=40 * MIB),
        name="rows_and_gram",
    )(partial)


def spread(x):
    x1 = x.astype(BF16).astype(F32)
    x2 = (x - x1).astype(BF16).astype(F32)
    return x1, x2, x - x1 - x2


def factor(gram):
    n = gram.shape[0]
    nb = PANEL
    lane = lax.broadcasted_iota(jnp.int32, (nb, n), 1)
    sub = lax.broadcasted_iota(jnp.int32, (nb, n), 0)
    eye = (lax.broadcasted_iota(jnp.int32, (n, n), 0) == lax.broadcasted_iota(jnp.int32, (n, n), 1)).astype(F32)
    left, right = gram, eye
    upper, inverse = [], []
    for p in range(n // nb):
        a = left[:nb]
        w = right[:nb]
        cols = [jnp.broadcast_to(a[:, p * nb + k:p * nb + k + 1], (nb, n)) for k in range(nb)]
        for j in range(nb):
            scale = lax.rsqrt(jnp.broadcast_to(cols[j][j:j + 1], (nb, n)))
            col = cols[j] * scale
            below = jnp.where(sub > j, col, 0.0)
            for k in range(j + 1, nb):
                cols[k] = cols[k] - below * jnp.broadcast_to(col[k:k + 1], (nb, n))
            a_row = jnp.broadcast_to(a[j:j + 1], (nb, n)) * scale
            w_row = jnp.broadcast_to(w[j:j + 1], (nb, n)) * scale
            a = jnp.where(sub == j, a_row, a - below * a_row)
            w = jnp.where(sub == j, w_row, w - below * w_row)
        upper.append(jnp.where(lane >= sub + p * nb, a, 0.0))
        inverse.append(w)
        rest = n - (p + 1) * nb
        if rest:
            a1, a2, a3 = spread(a)
            w1, w2, w3 = spread(w)
            lhs = jnp.concatenate([a1, a1, a2, a1, a2, a3], axis=0).T[n - rest:].astype(BF16)
            rhs_a = jnp.concatenate([a1, a2, a1, a3, a2, a1], axis=0)
            rhs_w = jnp.concatenate([w1, w2, w1, w3, w2, w1], axis=0)
            rhs = jnp.concatenate([rhs_a, rhs_w], axis=1).astype(BF16)
            change = jnp.dot(lhs, rhs, preferred_element_type=F32)
            left = left[nb:] - change[:, :n]
            right = right[nb:] - change[:, n:]
    return jnp.concatenate(upper, axis=0), jnp.concatenate(inverse, axis=0)


def basis_kernel(root, gram, rows, basis, r_factor, solve):
    @pl.when(pl.program_id(0) == 0)
    def _():
        upper, inverse = factor(gram[...])
        r_factor[...] = upper / root
        solve[...] = inverse * root

    width = rows.shape[1]
    x_hi, x_lo = split2(rows[...])
    s_hi, s_lo = split2(solve[...])
    both = lax.dot_general(x_hi, jnp.concatenate([s_hi, s_lo], axis=0), (((1,), (1,)), ((), ())),
                           preferred_element_type=F32)
    rest = lax.dot_general(x_lo, s_hi, (((1,), (1,)), ((), ())), preferred_element_type=F32)
    basis[...] = both[:, :width] + both[:, width:] + rest


def basis_of(gram, rows, root):
    part, width = rows.shape
    size = min(part, 1024)
    return pl.pallas_call(
        functools.partial(basis_kernel, root),
        out_shape=(jax.ShapeDtypeStruct((part, width), F32), jax.ShapeDtypeStruct((width, width), F32)),
        grid=(part // size,),
        in_specs=[
            pl.BlockSpec((width, width), lambda i: (0, 0)),
            pl.BlockSpec((size, width), lambda i: (i, 0)),
        ],
        out_specs=(
            pl.BlockSpec((size, width), lambda i: (i, 0)),
            pl.BlockSpec((width, width), lambda i: (0, 0)),
        ),
        scratch_shapes=[pltpu.VMEM((width, width), F32)],
        compiler_params=pltpu.CompilerParams(vmem_limit_bytes=24 * MIB),
        name="factor_and_basis",
    )(gram, rows)


def on_device(n_rows, n_cols, block_vector, op_tiles, tile_cols, live_counts):
    place = jnp.stack([lax.axis_index("rows"), lax.axis_index("cols")]).astype(jnp.int32)
    halo = relay(block_vector, n_rows, n_cols)
    partial = products(place, tile_cols, live_counts, block_vector, halo, op_tiles)
    rows, gram = rows_and_gram(partial, n_rows, n_cols)
    root = math.sqrt(block_vector.shape[0] * n_rows)
    return basis_of(gram, rows, root)


def solution(mesh):
    in_specs = (P("rows", None), P("rows", "cols", None, None), P("rows", "cols"), P("rows"))
    out_specs = (P(("rows", "cols"), None), P())
    return jax.shard_map(
        functools.partial(on_device, mesh.shape["rows"], mesh.shape["cols"]),
        mesh=mesh, in_specs=in_specs, out_specs=out_specs, check_vma=False,
    )
```

```python
import functools
import math

import jax
import jax.numpy as jnp
from jax import lax
from jax.experimental import pallas as pl
from jax.experimental.pallas import tpu as pltpu
from jax.sharding import PartitionSpec as P

MESH = pl.DeviceIdType.MESH
BF16 = jnp.bfloat16
F32 = jnp.float32
MIB = 1024 * 1024
PANEL = 16


def split2(x):
    hi = x.astype(BF16)
    lo = (x - hi.astype(F32)).astype(BF16)
    return hi, lo


def greet(peers):
    barrier = pltpu.get_barrier_semaphore()
    for cond, device in peers:
        if cond is None:
            pl.semaphore_signal(barrier, inc=1, device_id=device, device_id_type=MESH)
        else:
            @pl.when(cond)
            def _(device=device):
                pl.semaphore_signal(barrier, inc=1, device_id=device, device_id_type=MESH)
    total = 0
    for cond, _ in peers:
        total = total + (1 if cond is None else jnp.where(cond, 1, 0))
    pl.semaphore_wait(barrier, total)


def step_kernel(n_rows, n_cols, chunks, ahead, lag, pieces, cols, counts, own, tiles, rows_out, gram_out,
                own_v, halo, stage, a_hi, a_lo, out, got, acc, into,
                own_sem, stage_sem, rows_sem, near_s, near_r, far_s, far_r, sib_s, sib_r, part_s, part_r, sum_s, sum_r):
    r = lax.axis_index("rows")
    c = lax.axis_index("cols")
    blocks, slots, tile, _ = tiles.shape
    rows, width = blocks * tile, own.shape[2]
    odd = lax.rem(r, 2)
    partner = r + 1 - 2 * odd
    fwd_to = r + 2 - 4 * odd
    far_from = r - 2 + 4 * odd
    can_fwd = (fwd_to >= 0) & (fwd_to < n_rows)
    has_far = (far_from >= 0) & (far_from < n_rows)
    part = rows // n_cols
    size = part // chunks
    near_slot = 1 - odd
    far_slot = odd
    siblings = [(r, lax.rem(c + d, n_cols)) for d in range(1, n_cols)]
    steps = int(math.log2(n_rows))
    sum_peers = []
    for b in range(int(math.log2(n_cols))):
        bit = lax.rem(c // (1 << b), 2)
        sum_peers.append((r, c + (1 << b) * (1 - 2 * bit)))
    for b in range(steps):
        bit = lax.rem(r // (1 << b), 2)
        sum_peers.append((r + (1 << b) * (1 - 2 * bit), c))

    peers = [(None, (partner, c)), (can_fwd, (fwd_to, c)), (has_far, (far_from, c))]
    peers += [(None, device) for device in siblings]
    peers += [(None, device) for device in sum_peers[int(math.log2(n_cols)) + 1:]]

    def remote(src, dst, send_sem, recv_sem, device):
        return pltpu.make_async_remote_copy(
            src_ref=src, dst_ref=dst, send_sem=send_sem, recv_sem=recv_sem, device_id=device, device_id_type=MESH)

    def own_at(i, col):
        row = col * part + i * size
        return own.at[row // tile, pl.ds(pl.multiple_of(lax.rem(row, tile), size), size)]

    def halo_at(slot, i, col):
        row = col * part + i * size
        return halo.at[slot * blocks + row // tile, pl.ds(pl.multiple_of(lax.rem(row, tile), size), size)]

    def near(i):
        return remote(own_at(i, c), halo_at(odd, i, c), near_s.at[i], near_r.at[i], (partner, c))

    def near_in(i):
        return remote(own_at(i, c), halo_at(near_slot, i, c), near_s.at[i], near_r.at[i], (partner, c))

    def far(i):
        return remote(halo_at(near_slot, i, c), halo_at(far_slot, i, c),
                      far_s.at[i], far_r.at[i], (fwd_to, c))

    def sib(i, kind, d, incoming=False):
        slot = near_slot if kind == 0 else far_slot
        k = (kind * (n_cols - 1) + d - 1) * chunks + i
        col = lax.rem(c + n_cols - d, n_cols) if incoming else c
        return remote(halo_at(slot, i, c), halo_at(slot, i, col),
                      sib_s.at[k], sib_r.at[k], siblings[d - 1])

    group = blocks // chunks

    def fetch(i):
        k = lax.rem(i, 2)
        return pltpu.make_async_copy(tiles.at[pl.ds(i * group, group)], stage.at[k], stage_sem.at[k])

    bring_own = pltpu.make_async_copy(own, own_v, own_sem)
    bring_own.start()
    fetch(0).start()
    greet(peers)
    for i in range(ahead):
        near(i).start()

    before = (r - 1) * blocks
    first_slot = c * slots

    def picked(row, ours):
        live = counts[row] - first_slot
        parts = []
        for s in range(slots):
            rel = cols[row, s] - before
            after_prev = (rel >= blocks).astype(jnp.int32)
            after_own = (rel >= 2 * blocks).astype(jnp.int32)
            mine = after_prev - after_own
            alive = (live > s).astype(jnp.int32)
            if ours:
                use = mine * alive
                at = use * (rel - blocks)
                b = own_v[lax.max(lax.min(at, blocks - 1), 0)]
            else:
                use = (1 - mine) * alive
                at = use * (rel - blocks * after_own) + (1 - use) * (near_slot * blocks)
                b = halo[lax.max(lax.min(at, 2 * blocks - 1), 0)]
            parts.append(b * use.astype(F32))
        return split2(jnp.concatenate(parts, axis=0))

    def times(hi, lo, b_hi, b_lo):
        both = jnp.dot(hi, jnp.concatenate([b_hi, b_lo], axis=1), preferred_element_type=F32)
        return both[:, :width] + both[:, width:] + jnp.dot(lo, b_hi, preferred_element_type=F32)

    def at_block(row):
        return pl.ds(pl.multiple_of(row * tile, tile), tile)

    def own_products(i):
        k = lax.rem(i, 2)
        fetch(i).wait()

        @pl.when(i + 1 < chunks)
        def _():
            fetch(i + 1).start()

        for j in range(group):
            row = i * group + j
            hi, lo = split2(jnp.concatenate([stage[k, j, s] for s in range(slots)], axis=1))
            a_hi[row] = hi
            a_lo[row] = lo
            b_hi, b_lo = picked(row, True)
            out[at_block(row), :] = times(hi, lo, b_hi, b_lo)

    def halo_products(at_rows):
        sums = []
        for row in at_rows:
            b_hi, b_lo = picked(row, False)
            sums.append(out[at_block(row), :] + times(a_hi[row], a_lo[row], b_hi, b_lo))
        for row, total in zip(at_rows, sums):
            out[at_block(row), :] = total

    @pl.loop(0, chunks + lag)
    def _(i):
        @pl.when(i < chunks)
        def _():
            near_in(i).wait_recv()

            @pl.when(can_fwd)
            def _():
                far(i).start()

            for d in range(1, n_cols):
                sib(i, 0, d).start()

            @pl.when(i + ahead < chunks)
            def _():
                near(i + ahead).start()

        @pl.when((i >= lag) & has_far)
        def _():
            far(i - lag).wait_recv()
            for d in range(1, n_cols):
                sib(i - lag, 1, d).start()

        @pl.when(i == 0)
        def _():
            bring_own.wait()

        @pl.when(i < chunks)
        def _():
            own_products(i)

    @pl.loop(0, chunks)
    def _(i):
        for d in range(1, n_cols):
            sib(i, 0, d, True).wait_recv()
            sib(i, 0, d).wait_send()

        @pl.when(has_far)
        def _():
            for d in range(1, n_cols):
                sib(i, 1, d, True).wait_recv()
                sib(i, 1, d).wait_send()

        near(i).wait_send()

        @pl.when(can_fwd)
        def _():
            far(i).wait_send()

    piece = part // pieces
    piece_blocks = piece // tile
    unroll = 2 if piece_blocks % 2 == 0 else 1

    def multiply_piece(col, i):
        first = col * (part // tile) + i * piece_blocks

        @pl.loop(0, piece_blocks // unroll)
        def _(j):
            halo_products([first + j * unroll + u for u in range(unroll)])

    def piece_span(col, i):
        return pl.ds(pl.multiple_of(col * part + i * piece, piece), piece)

    def give(i, d):
        k = (d - 1) * pieces + i
        return remote(out.at[piece_span(lax.rem(c + d, n_cols), i)], got.at[d - 1, piece_span(0, i)],
                      part_s.at[k], part_r.at[k], siblings[d - 1])

    def keep(i):
        return pltpu.make_async_copy(out.at[piece_span(c, i)], rows_out.at[piece_span(0, i)], rows_sem.at[i])

    for d in range(1, n_cols):
        @pl.loop(0, pieces)
        def _(i, d=d):
            multiply_piece(lax.rem(c + d, n_cols), i)
            give(i, d).start()

    acc[0] = jnp.zeros_like(acc.at[0])

    @pl.loop(0, pieces)
    def _(i):
        multiply_piece(c, i)
        x = out[piece_span(c, i), :]
        for d in range(1, n_cols):
            give(i, d).wait_recv()
            x = x + got[d - 1, piece_span(0, i), :]
        out[piece_span(c, i), :] = x
        keep(i).start()
        hi, lo = split2(x)
        both = jnp.concatenate([hi, lo], axis=1)
        g = lax.dot_general(both, both, (((0,), (0,)), ((), ())), preferred_element_type=F32)
        acc[0] += (g[:width, :width] + g[width:, width:]) + (g[:width, width:] + g[width:, :width])

    def add_up(s):
        return remote(acc.at[s], into.at[s], sum_s.at[s], sum_r.at[s], sum_peers[s])

    for s in range(len(sum_peers)):
        add_up(s).start()
        add_up(s).wait_recv()
        acc[s + 1] = acc[s] + into[s]
    gram_out[...] = acc[len(sum_peers)]

    for s in range(len(sum_peers)):
        add_up(s).wait_send()

    @pl.loop(0, pieces)
    def _(i):
        keep(i).wait()
        for d in range(1, n_cols):
            give(i, d).wait_send()


def rows_and_gram(tile_cols, live_counts, block_vector, op_tiles, n_rows, n_cols):
    rows, width = block_vector.shape
    blocks, slots, tile, _ = op_tiles.shape
    part = rows // n_cols
    chunks = min(32, blocks)
    while part // chunks > tile:
        chunks *= 2
    pieces = 4
    sums = int(math.log2(n_rows * n_cols))
    n_sib = max(1, 2 * (n_cols - 1) * chunks)
    n_give = max(1, (n_cols - 1) * pieces)
    dma = pltpu.SemaphoreType.DMA
    vmem = pl.BlockSpec(memory_space=pltpu.VMEM)
    smem = pl.BlockSpec(memory_space=pltpu.SMEM)
    hbm = pl.BlockSpec(memory_space=pl.ANY)
    return pl.pallas_call(
        functools.partial(step_kernel, n_rows, n_cols, chunks, 8, 2, pieces),
        out_shape=(jax.ShapeDtypeStruct((part, width), F32), jax.ShapeDtypeStruct((width, width), F32)),
        in_specs=[smem, smem, hbm, hbm],
        out_specs=(hbm, vmem),
        scratch_shapes=[
            pltpu.VMEM((blocks, tile, width), F32),
            pltpu.VMEM((2 * blocks, tile, width), F32),
            pltpu.VMEM((2, blocks // chunks, slots, tile, tile), F32),
            pltpu.VMEM((blocks, tile, slots * tile), BF16),
            pltpu.VMEM((blocks, tile, slots * tile), BF16),
            pltpu.VMEM((rows, width), F32),
            pltpu.VMEM((max(1, n_cols - 1), part, width), F32),
            pltpu.VMEM((sums + 1, width, width), F32),
            pltpu.VMEM((sums, width, width), F32),
            dma, dma((2,)), dma((pieces,)),
            dma((chunks,)), dma((chunks,)), dma((chunks,)), dma((chunks,)), dma((n_sib,)), dma((n_sib,)),
            dma((n_give,)), dma((n_give,)), dma((sums,)), dma((sums,)),
        ],
        compiler_params=pltpu.CompilerParams(collective_id=0, has_side_effects=True, vmem_limit_bytes=48 * MIB),
        name="rows_and_gram",
    )(tile_cols, live_counts, block_vector.reshape(blocks, tile, width), op_tiles)


def spread(x):
    x1 = x.astype(BF16).astype(F32)
    x2 = (x - x1).astype(BF16).astype(F32)
    return x1, x2, x - x1 - x2


def factor(gram):
    n = gram.shape[0]
    nb = PANEL
    lane = lax.broadcasted_iota(jnp.int32, (nb, n), 1)
    sub = lax.broadcasted_iota(jnp.int32, (nb, n), 0)
    eye = (lax.broadcasted_iota(jnp.int32, (n, n), 0) == lax.broadcasted_iota(jnp.int32, (n, n), 1)).astype(F32)
    left, right = gram, eye
    upper, inverse = [], []
    for p in range(n // nb):
        a = left[:nb]
        w = right[:nb]
        cols = [jnp.broadcast_to(a[:, p * nb + k:p * nb + k + 1], (nb, n)) for k in range(nb)]
        for j in range(nb):
            scale = lax.rsqrt(jnp.broadcast_to(cols[j][j:j + 1], (nb, n)))
            col = cols[j] * scale
            below = jnp.where(sub > j, col, 0.0)
            for k in range(j + 1, nb):
                cols[k] = cols[k] - below * jnp.broadcast_to(col[k:k + 1], (nb, n))
            a_row = jnp.broadcast_to(a[j:j + 1], (nb, n)) * scale
            w_row = jnp.broadcast_to(w[j:j + 1], (nb, n)) * scale
            a = jnp.where(sub == j, a_row, a - below * a_row)
            w = jnp.where(sub == j, w_row, w - below * w_row)
        upper.append(jnp.where(lane >= sub + p * nb, a, 0.0))
        inverse.append(w)
        rest = n - (p + 1) * nb
        if rest:
            a1, a2, a3 = spread(a)
            w1, w2, w3 = spread(w)
            lhs = jnp.concatenate([a1, a1, a2, a1, a2, a3], axis=0).T[n - rest:].astype(BF16)
            rhs_a = jnp.concatenate([a1, a2, a1, a3, a2, a1], axis=0)
            rhs_w = jnp.concatenate([w1, w2, w1, w3, w2, w1], axis=0)
            rhs = jnp.concatenate([rhs_a, rhs_w], axis=1).astype(BF16)
            change = jnp.dot(lhs, rhs, preferred_element_type=F32)
            left = left[nb:] - change[:, :n]
            right = right[nb:] - change[:, n:]
    return jnp.concatenate(upper, axis=0), jnp.concatenate(inverse, axis=0)


def basis_kernel(root, gram, rows, basis, r_factor, solve):
    @pl.when(pl.program_id(0) == 0)
    def _():
        upper, inverse = factor(gram[...])
        r_factor[...] = upper / root
        solve[...] = inverse * root

    width = rows.shape[1]
    x_hi, x_lo = split2(rows[...])
    s_hi, s_lo = split2(solve[...])
    both = lax.dot_general(x_hi, jnp.concatenate([s_hi, s_lo], axis=0), (((1,), (1,)), ((), ())),
                           preferred_element_type=F32)
    rest = lax.dot_general(x_lo, s_hi, (((1,), (1,)), ((), ())), preferred_element_type=F32)
    basis[...] = both[:, :width] + both[:, width:] + rest


def basis_of(gram, rows, root):
    part, width = rows.shape
    size = min(part, 1024)
    return pl.pallas_call(
        functools.partial(basis_kernel, root),
        out_shape=(jax.ShapeDtypeStruct((part, width), F32), jax.ShapeDtypeStruct((width, width), F32)),
        grid=(part // size,),
        in_specs=[
            pl.BlockSpec((width, width), lambda i: (0, 0)),
            pl.BlockSpec((size, width), lambda i: (i, 0)),
        ],
        out_specs=(
            pl.BlockSpec((size, width), lambda i: (i, 0)),
            pl.BlockSpec((width, width), lambda i: (0, 0)),
        ),
        scratch_shapes=[pltpu.VMEM((width, width), F32)],
        compiler_params=pltpu.CompilerParams(vmem_limit_bytes=24 * MIB),
        name="factor_and_basis",
    )(gram, rows)


def on_device(n_rows, n_cols, block_vector, op_tiles, tile_cols, live_counts):
    rows, gram = rows_and_gram(tile_cols, live_counts, block_vector, op_tiles, n_rows, n_cols)
    root = math.sqrt(block_vector.shape[0] * n_rows)
    return basis_of(gram, rows, root)


def solution(mesh):
    in_specs = (P("rows", None), P("rows", "cols", None, None), P("rows", "cols"), P("rows"))
    out_specs = (P(("rows", "cols"), None), P())
    return jax.shard_map(
        functools.partial(on_device, mesh.shape["rows"], mesh.shape["cols"]),
        mesh=mesh, in_specs=in_specs, out_specs=out_specs, check_vma=False,
    )
```

```python
import functools
import math

import jax
import jax.numpy as jnp
from jax import lax
from jax.experimental import pallas as pl
from jax.experimental.pallas import tpu as pltpu
from jax.sharding import PartitionSpec as P

MESH = pl.DeviceIdType.MESH
BF16 = jnp.bfloat16
F32 = jnp.float32
MIB = 1024 * 1024
PANEL = 16


def split2(x):
    hi = x.astype(BF16)
    lo = (x - hi.astype(F32)).astype(BF16)
    return hi, lo


def greet(peers):
    barrier = pltpu.get_barrier_semaphore()
    for cond, device in peers:
        if cond is None:
            pl.semaphore_signal(barrier, inc=1, device_id=device, device_id_type=MESH)
        else:
            @pl.when(cond)
            def _(device=device):
                pl.semaphore_signal(barrier, inc=1, device_id=device, device_id_type=MESH)
    total = 0
    for cond, _ in peers:
        total = total + (1 if cond is None else jnp.where(cond, 1, 0))
    pl.semaphore_wait(barrier, total)


def step_kernel(n_rows, n_cols, chunks, ahead, lag, pieces, cols, counts, own, tiles, rows_out, gram_out,
                own_v, own_split, halo, halo_split, stage, a_split, out, got, gram, halves, acc, into, full,
                own_sem, stage_sem, rows_sem, near_s, near_r, far_s, far_r, sib_s, sib_r, part_s, part_r,
                half_s, half_r, sum_s, sum_r, full_s, full_r):
    r = lax.axis_index("rows")
    c = lax.axis_index("cols")
    blocks, slots, tile, _ = tiles.shape
    rows, width = blocks * tile, own.shape[2]
    odd = lax.rem(r, 2)
    partner = r + 1 - 2 * odd
    fwd_to = r + 2 - 4 * odd
    far_from = r - 2 + 4 * odd
    can_fwd = (fwd_to >= 0) & (fwd_to < n_rows)
    has_far = (far_from >= 0) & (far_from < n_rows)
    part = rows // n_cols
    part_blocks = part // tile
    size = part // chunks
    near_slot = 1 - odd
    far_slot = odd
    siblings = [(r, lax.rem(c + d, n_cols)) for d in range(1, n_cols)]
    sum_peers = []
    for b in range(int(math.log2(n_rows))):
        bit = lax.rem(r // (1 << b), 2)
        sum_peers.append((r + (1 << b) * (1 - 2 * bit), c))

    peers = [(None, (partner, c)), (can_fwd, (fwd_to, c)), (has_far, (far_from, c))]
    peers += [(None, device) for device in siblings]
    peers += [(None, device) for device in sum_peers[1:]]

    def remote(src, dst, send_sem, recv_sem, device):
        return pltpu.make_async_remote_copy(
            src_ref=src, dst_ref=dst, send_sem=send_sem, recv_sem=recv_sem, device_id=device, device_id_type=MESH)

    def chunk_place(i, col):
        row = col * part + i * size
        return row // tile, pl.ds(pl.multiple_of(lax.rem(row, tile), size), size)

    def own_at(i, col):
        block, span = chunk_place(i, col)
        return own.at[block, span]

    def halo_at(slot, i, col):
        block, span = chunk_place(i, col)
        return halo.at[slot * blocks + block, span]

    def near(i):
        return remote(own_at(i, c), halo_at(odd, i, c), near_s, near_r.at[i], (partner, c))

    def near_in(i):
        return remote(own_at(i, c), halo_at(near_slot, i, c), near_s, near_r.at[i], (partner, c))

    def far(i):
        return remote(halo_at(near_slot, i, c), halo_at(far_slot, i, c), far_s, far_r.at[i], (fwd_to, c))

    def sib(i, kind, d, incoming=False):
        slot = near_slot if kind == 0 else far_slot
        k = (kind * (n_cols - 1) + d - 1) * chunks + i
        col = lax.rem(c + n_cols - d, n_cols) if incoming else c
        return remote(halo_at(slot, i, c), halo_at(slot, i, col),
                      sib_s.at[kind * (n_cols - 1) + d - 1], sib_r.at[k], siblings[d - 1])

    def all_sent(sem, device):
        whole = halo.at[pl.ds(near_slot * blocks + c * part_blocks, part_blocks)]
        remote(whole, whole, sem, near_r.at[0], device).wait_send()

    group = blocks // chunks

    def fetch(i):
        k = lax.rem(i, 2)
        return pltpu.make_async_copy(tiles.at[pl.ds(i * group, group)], stage.at[k], stage_sem.at[k])

    bring_own = pltpu.make_async_copy(own, own_v, own_sem)
    bring_own.start()
    fetch(0).start()
    greet(peers)
    for i in range(ahead):
        near(i).start()

    def split_halo(slot, i, col):
        block, span = chunk_place(i, col)
        hi, lo = split2(halo[slot * blocks + block, span, :])
        halo_split[slot * blocks + block, span, :] = jnp.concatenate([hi, lo], axis=1)

    own_split[blocks] = jnp.zeros((tile, 2 * width), BF16)
    halo_split[2 * blocks] = jnp.zeros((tile, 2 * width), BF16)
    bring_own.wait()

    @pl.loop(0, blocks)
    def _(i):
        hi, lo = split2(own_v[i])
        own_split[i] = jnp.concatenate([hi, lo], axis=1)

    before = (r - 1) * blocks
    first_slot = c * slots

    def picked(row, ours):
        live = counts[row] - first_slot
        parts = []
        for s in range(slots):
            rel = cols[s, row] - before
            after_prev = (rel >= blocks).astype(jnp.int32)
            after_own = (rel >= 2 * blocks).astype(jnp.int32)
            mine = after_prev - after_own
            alive = (live > s).astype(jnp.int32)
            if ours:
                use = mine * alive
                at = use * (rel - blocks) + (1 - use) * blocks
                parts.append(own_split[lax.max(lax.min(at, blocks), 0)])
            else:
                use = (1 - mine) * alive
                at = use * (rel - blocks * after_own) + (1 - use) * (2 * blocks)
                parts.append(halo_split[lax.max(lax.min(at, 2 * blocks), 0)])
        return jnp.concatenate(parts, axis=0)

    def times(a, b):
        p = jnp.dot(a, b, preferred_element_type=F32)
        return (p[:tile, :width] + p[tile:, width:]) + (p[:tile, width:] + p[tile:, :width])

    def at_block(row):
        return pl.ds(pl.multiple_of(row * tile, tile), tile)

    def own_products(i):
        k = lax.rem(i, 2)
        fetch(i).wait()

        @pl.when(i + 1 < chunks)
        def _():
            fetch(i + 1).start()

        for j in range(group):
            row = i * group + j
            hi, lo = split2(jnp.concatenate([stage[k, j, s] for s in range(slots)], axis=1))
            a = jnp.concatenate([hi, lo], axis=0)
            a_split[row] = a
            out[at_block(row), :] = times(a, picked(row, True))

    def halo_products(at_rows):
        sums = [out[at_block(row), :] + times(a_split[row], picked(row, False)) for row in at_rows]
        for row, total in zip(at_rows, sums):
            out[at_block(row), :] = total

    @pl.loop(0, chunks + 2 * lag)
    def _(i):
        @pl.when(i < chunks)
        def _():
            near_in(i).wait_recv()

            @pl.when(can_fwd)
            def _():
                far(i).start()

            for d in range(1, n_cols):
                sib(i, 0, d).start()

            @pl.when(i + ahead < chunks)
            def _():
                near(i + ahead).start()

            split_halo(near_slot, i, c)

        @pl.when((i >= lag) & (i < chunks + lag) & has_far)
        def _():
            far(i - lag).wait_recv()
            for d in range(1, n_cols):
                sib(i - lag, 1, d).start()
            split_halo(far_slot, i - lag, c)

        @pl.when((i >= lag) & (i < chunks + lag))
        def _():
            for d in range(1, n_cols):
                sib(i - lag, 0, d, True).wait_recv()
                split_halo(near_slot, i - lag, lax.rem(c + n_cols - d, n_cols))

        @pl.when((i >= 2 * lag) & has_far)
        def _():
            for d in range(1, n_cols):
                sib(i - 2 * lag, 1, d, True).wait_recv()
                split_halo(far_slot, i - 2 * lag, lax.rem(c + n_cols - d, n_cols))

        @pl.when(i < chunks)
        def _():
            own_products(i)

    piece = part // pieces
    piece_blocks = piece // tile
    unroll = 2 if piece_blocks % 2 == 0 else 1

    def multiply_piece(col, i):
        first = col * part_blocks + i * piece_blocks

        @pl.loop(0, piece_blocks // unroll)
        def _(j):
            halo_products([first + j * unroll + u for u in range(unroll)])

    def piece_span(col, i):
        return pl.ds(pl.multiple_of(col * part + i * piece, piece), piece)

    def give(i, d):
        k = (d - 1) * pieces + i
        return remote(out.at[piece_span(lax.rem(c + d, n_cols), i)], got.at[d - 1, piece_span(0, i)],
                      part_s.at[k], part_r.at[k], siblings[d - 1])

    def keep(i):
        return pltpu.make_async_copy(out.at[piece_span(c, i)], rows_out.at[piece_span(0, i)], rows_sem.at[i])

    for d in range(1, n_cols):
        @pl.loop(0, pieces)
        def _(i, d=d):
            multiply_piece(lax.rem(c + d, n_cols), i)
            give(i, d).start()

    gram[...] = jnp.zeros_like(gram)

    @pl.loop(0, pieces)
    def _(i):
        multiply_piece(c, i)
        x = out[piece_span(c, i), :]
        for d in range(1, n_cols):
            give(i, d).wait_recv()
            x = x + got[d - 1, piece_span(0, i), :]
        out[piece_span(c, i), :] = x
        keep(i).start()
        hi, lo = split2(x)
        gram[...] += lax.dot_general(hi, jnp.concatenate([hi, lo], axis=1), (((0,), (0,)), ((), ())),
                                     preferred_element_type=F32)

    cross = gram[:, width:]
    gram[:, :width] = gram[:, :width] + (cross + cross.T)

    half = width // n_cols

    def half_span(col):
        return pl.ds(pl.multiple_of(col * half, half), half)

    def give_half(d):
        return remote(gram.at[half_span(lax.rem(c + d, n_cols)), pl.ds(0, width)], halves.at[d - 1],
                      half_s.at[d - 1], half_r.at[d - 1], siblings[d - 1])

    for d in range(1, n_cols):
        give_half(d).start()
    total = gram[half_span(c), pl.ds(0, width)]
    for d in range(1, n_cols):
        give_half(d).wait_recv()
        total = total + halves[d - 1]
    acc[0] = total

    def add_up(s):
        return remote(acc.at[s], into.at[s], sum_s.at[s], sum_r.at[s], sum_peers[s])

    n_sums = len(sum_peers)
    for s in range(n_sums):
        add_up(s).start()
        add_up(s).wait_recv()
        acc[s + 1] = acc[s] + into[s]

    def hand_out(d):
        return remote(acc.at[n_sums], full.at[half_span(c)], full_s.at[d - 1], full_r.at[d - 1], siblings[d - 1])

    def hand_in(d):
        return remote(acc.at[n_sums], full.at[half_span(lax.rem(c + n_cols - d, n_cols))],
                      full_s.at[d - 1], full_r.at[d - 1], siblings[d - 1])

    for d in range(1, n_cols):
        hand_out(d).start()

    all_sent(near_s, (partner, c))

    @pl.when(can_fwd)
    def _():
        all_sent(far_s, (fwd_to, c))

    for d in range(1, n_cols):
        all_sent(sib_s.at[d - 1], siblings[d - 1])

        @pl.when(has_far)
        def _(d=d):
            all_sent(sib_s.at[n_cols - 1 + d - 1], siblings[d - 1])

        give_half(d).wait_send()
        for i in range(pieces):
            give(i, d).wait_send()
    for s in range(n_sums):
        add_up(s).wait_send()
    for i in range(pieces):
        keep(i).wait()
    full[half_span(c), :] = acc[n_sums]
    for d in range(1, n_cols):
        hand_in(d).wait_recv()
        hand_out(d).wait_send()
    gram_out[...] = full[...]


def rows_and_gram(tile_cols, live_counts, block_vector, op_tiles, n_rows, n_cols):
    rows, width = block_vector.shape
    blocks, slots, tile, _ = op_tiles.shape
    part = rows // n_cols
    chunks = min(32, blocks)
    while part // chunks > tile:
        chunks *= 2
    pieces = 4
    sums = int(math.log2(n_rows))
    others = max(1, n_cols - 1)
    dma = pltpu.SemaphoreType.DMA
    vmem = pl.BlockSpec(memory_space=pltpu.VMEM)
    smem = pl.BlockSpec(memory_space=pltpu.SMEM)
    hbm = pl.BlockSpec(memory_space=pl.ANY)
    return pl.pallas_call(
        functools.partial(step_kernel, n_rows, n_cols, chunks, 8, 2, pieces),
        out_shape=(jax.ShapeDtypeStruct((part, width), F32), jax.ShapeDtypeStruct((width, width), F32)),
        in_specs=[smem, smem, hbm, hbm],
        out_specs=(hbm, vmem),
        scratch_shapes=[
            pltpu.VMEM((blocks, tile, width), F32),
            pltpu.VMEM((blocks + 1, tile, 2 * width), BF16),
            pltpu.VMEM((2 * blocks, tile, width), F32),
            pltpu.VMEM((2 * blocks + 1, tile, 2 * width), BF16),
            pltpu.VMEM((2, blocks // chunks, slots, tile, tile), F32),
            pltpu.VMEM((blocks, 2 * tile, slots * tile), BF16),
            pltpu.VMEM((rows, width), F32),
            pltpu.VMEM((others, part, width), F32),
            pltpu.VMEM((width, 2 * width), F32),
            pltpu.VMEM((others, width // n_cols, width), F32),
            pltpu.VMEM((sums + 1, width // n_cols, width), F32),
            pltpu.VMEM((sums, width // n_cols, width), F32),
            pltpu.VMEM((width, width), F32),
            dma, dma((2,)), dma((pieces,)),
            dma, dma((chunks,)), dma, dma((chunks,)), dma((2 * others,)), dma((2 * others * chunks,)),
            dma((others * pieces,)), dma((others * pieces,)),
            dma((others,)), dma((others,)), dma((sums,)), dma((sums,)), dma((others,)), dma((others,)),
        ],
        compiler_params=pltpu.CompilerParams(collective_id=0, has_side_effects=True, vmem_limit_bytes=56 * MIB),
        name="rows_and_gram",
    )(tile_cols.T, live_counts, block_vector.reshape(blocks, tile, width), op_tiles)


def spread(x):
    x1 = x.astype(BF16).astype(F32)
    x2 = (x - x1).astype(BF16).astype(F32)
    return x1, x2, x - x1 - x2


def factor(gram):
    n = gram.shape[0]
    nb = PANEL
    lane = lax.broadcasted_iota(jnp.int32, (nb, n), 1)
    sub = lax.broadcasted_iota(jnp.int32, (nb, n), 0)
    eye = (lax.broadcasted_iota(jnp.int32, (n, n), 0) == lax.broadcasted_iota(jnp.int32, (n, n), 1)).astype(F32)
    left, right = gram, eye
    upper, inverse = [], []
    for p in range(n // nb):
        a = left[:nb]
        w = right[:nb]
        cols = [jnp.broadcast_to(a[:, p * nb + k:p * nb + k + 1], (nb, n)) for k in range(nb)]
        for j in range(nb):
            scale = lax.rsqrt(jnp.broadcast_to(cols[j][j:j + 1], (nb, n)))
            col = cols[j] * scale
            below = jnp.where(sub > j, col, 0.0)
            for k in range(j + 1, nb):
                cols[k] = cols[k] - below * jnp.broadcast_to(col[k:k + 1], (nb, n))
            a_row = jnp.broadcast_to(a[j:j + 1], (nb, n)) * scale
            w_row = jnp.broadcast_to(w[j:j + 1], (nb, n)) * scale
            a = jnp.where(sub == j, a_row, a - below * a_row)
            w = jnp.where(sub == j, w_row, w - below * w_row)
        upper.append(jnp.where(lane >= sub + p * nb, a, 0.0))
        inverse.append(w)
        rest = n - (p + 1) * nb
        if rest:
            a1, a2, a3 = spread(a)
            w1, w2, w3 = spread(w)
            lhs = jnp.concatenate([a1, a1, a2, a1, a2, a3], axis=0).T[n - rest:].astype(BF16)
            rhs_a = jnp.concatenate([a1, a2, a1, a3, a2, a1], axis=0)
            rhs_w = jnp.concatenate([w1, w2, w1, w3, w2, w1], axis=0)
            rhs = jnp.concatenate([rhs_a, rhs_w], axis=1).astype(BF16)
            change = jnp.dot(lhs, rhs, preferred_element_type=F32)
            left = left[nb:] - change[:, :n]
            right = right[nb:] - change[:, n:]
    return jnp.concatenate(upper, axis=0), jnp.concatenate(inverse, axis=0)


def basis_kernel(root, gram, rows, basis, r_factor, solve):
    @pl.when(pl.program_id(0) == 0)
    def _():
        upper, inverse = factor(gram[...])
        r_factor[...] = upper / root
        solve[...] = inverse * root

    width = rows.shape[1]
    x_hi, x_lo = split2(rows[...])
    s_hi, s_lo = split2(solve[...])
    both = lax.dot_general(x_hi, jnp.concatenate([s_hi, s_lo], axis=0), (((1,), (1,)), ((), ())),
                           preferred_element_type=F32)
    rest = lax.dot_general(x_lo, s_hi, (((1,), (1,)), ((), ())), preferred_element_type=F32)
    basis[...] = both[:, :width] + both[:, width:] + rest


def basis_of(gram, rows, root):
    part, width = rows.shape
    size = min(part, 1024)
    return pl.pallas_call(
        functools.partial(basis_kernel, root),
        out_shape=(jax.ShapeDtypeStruct((part, width), F32), jax.ShapeDtypeStruct((width, width), F32)),
        grid=(part // size,),
        in_specs=[
            pl.BlockSpec((width, width), lambda i: (0, 0)),
            pl.BlockSpec((size, width), lambda i: (i, 0)),
        ],
        out_specs=(
            pl.BlockSpec((size, width), lambda i: (i, 0)),
            pl.BlockSpec((width, width), lambda i: (0, 0)),
        ),
        scratch_shapes=[pltpu.VMEM((width, width), F32)],
        compiler_params=pltpu.CompilerParams(vmem_limit_bytes=24 * MIB),
        name="factor_and_basis",
    )(gram, rows)


def on_device(n_rows, n_cols, block_vector, op_tiles, tile_cols, live_counts):
    rows, gram = rows_and_gram(tile_cols, live_counts, block_vector, op_tiles, n_rows, n_cols)
    root = math.sqrt(block_vector.shape[0] * n_rows)
    return basis_of(gram, rows, root)


def solution(mesh):
    in_specs = (P("rows", None), P("rows", "cols", None, None), P("rows", "cols"), P("rows"))
    out_specs = (P(("rows", "cols"), None), P())
    return jax.shard_map(
        functools.partial(on_device, mesh.shape["rows"], mesh.shape["cols"]),
        mesh=mesh, in_specs=in_specs, out_specs=out_specs, check_vma=False,
    )
```

```python
import functools
import math

import jax
import jax.numpy as jnp
from jax import lax
from jax.experimental import pallas as pl
from jax.experimental.pallas import tpu as pltpu
from jax.sharding import PartitionSpec as P

MESH = pl.DeviceIdType.MESH
BF16 = jnp.bfloat16
F32 = jnp.float32
MIB = 1024 * 1024
PANEL = 16


def split2(x):
    hi = x.astype(BF16)
    lo = (x - hi.astype(F32)).astype(BF16)
    return hi, lo


def greet(peers):
    barrier = pltpu.get_barrier_semaphore()
    for cond, device in peers:
        if cond is None:
            pl.semaphore_signal(barrier, inc=1, device_id=device, device_id_type=MESH)
        else:
            @pl.when(cond)
            def _(device=device):
                pl.semaphore_signal(barrier, inc=1, device_id=device, device_id_type=MESH)
    total = 0
    for cond, _ in peers:
        total = total + (1 if cond is None else jnp.where(cond, 1, 0))
    pl.semaphore_wait(barrier, total)


def step_kernel(n_rows, n_cols, chunks, ahead, lag, pieces, cols, counts, own, tiles, rows_out, gram_out,
                own_split, halo, halo_split, stage, a_split, out, got, gram, halves, acc, into, full,
                own_sem, stage_sem, rows_sem, near_s, near_r, far_s, far_r, sib_s, sib_r, part_s, part_r,
                half_s, half_r, sum_s, sum_r, full_s, full_r):
    r = lax.axis_index("rows")
    c = lax.axis_index("cols")
    blocks, slots, tile, _ = tiles.shape
    rows, width = blocks * tile, own.shape[2]
    odd = lax.rem(r, 2)
    partner = r + 1 - 2 * odd
    fwd_to = r + 2 - 4 * odd
    far_from = r - 2 + 4 * odd
    can_fwd = (fwd_to >= 0) & (fwd_to < n_rows)
    has_far = (far_from >= 0) & (far_from < n_rows)
    part = rows // n_cols
    part_blocks = part // tile
    size = part // chunks
    near_slot = 1 - odd
    far_slot = odd
    siblings = [(r, lax.rem(c + d, n_cols)) for d in range(1, n_cols)]
    sum_peers = []
    for b in range(int(math.log2(n_rows))):
        bit = lax.rem(r // (1 << b), 2)
        sum_peers.append((r + (1 << b) * (1 - 2 * bit), c))

    peers = [(None, (partner, c)), (can_fwd, (fwd_to, c)), (has_far, (far_from, c))]
    peers += [(None, device) for device in siblings]
    peers += [(None, device) for device in sum_peers[1:]]

    def remote(src, dst, send_sem, recv_sem, device):
        return pltpu.make_async_remote_copy(
            src_ref=src, dst_ref=dst, send_sem=send_sem, recv_sem=recv_sem, device_id=device, device_id_type=MESH)

    def chunk_place(i, col):
        row = col * part + i * size
        return row // tile, pl.ds(pl.multiple_of(lax.rem(row, tile), size), size)

    def own_at(i, col):
        block, span = chunk_place(i, col)
        return own.at[block, span]

    def halo_at(slot, i, col):
        block, span = chunk_place(i, col)
        return halo.at[slot * blocks + block, span]

    def near(i):
        return remote(own_at(i, c), halo_at(odd, i, c), near_s, near_r.at[i], (partner, c))

    def near_in(i):
        return remote(own_at(i, c), halo_at(near_slot, i, c), near_s, near_r.at[i], (partner, c))

    def far(i):
        return remote(halo_at(near_slot, i, c), halo_at(far_slot, i, c), far_s, far_r.at[i], (fwd_to, c))

    def sib(i, kind, d, incoming=False):
        slot = near_slot if kind == 0 else far_slot
        k = (kind * (n_cols - 1) + d - 1) * chunks + i
        col = lax.rem(c + n_cols - d, n_cols) if incoming else c
        return remote(halo_at(slot, i, c), halo_at(slot, i, col),
                      sib_s.at[kind * (n_cols - 1) + d - 1], sib_r.at[k], siblings[d - 1])

    def all_sent(sem, device):
        whole = halo.at[pl.ds(near_slot * blocks + c * part_blocks, part_blocks)]
        remote(whole, whole, sem, near_r.at[0], device).wait_send()

    group = blocks // chunks

    def fetch(i):
        k = lax.rem(i, 2)
        return pltpu.make_async_copy(tiles.at[pl.ds(i * group, group)], stage.at[k], stage_sem.at[k])

    bring_own = pltpu.make_async_copy(own, out, own_sem)
    bring_own.start()
    fetch(0).start()
    greet(peers)
    for i in range(ahead):
        near(i).start()

    def split_halo(slot, i, col):
        block, span = chunk_place(i, col)
        hi, lo = split2(halo[slot * blocks + block, span, :])
        halo_split[slot * blocks + block, span, :] = jnp.concatenate([hi, lo], axis=1)

    own_split[blocks] = jnp.zeros((tile, 2 * width), BF16)
    halo_split[2 * blocks] = jnp.zeros((tile, 2 * width), BF16)
    bring_own.wait()

    @pl.loop(0, blocks)
    def _(i):
        hi, lo = split2(out[i])
        own_split[i] = jnp.concatenate([hi, lo], axis=1)

    before = (r - 1) * blocks
    first_slot = c * slots

    def picked(row, ours):
        live = counts[row] - first_slot
        parts = []
        for s in range(slots):
            rel = cols[s, row] - before
            after_prev = (rel >= blocks).astype(jnp.int32)
            after_own = (rel >= 2 * blocks).astype(jnp.int32)
            mine = after_prev - after_own
            alive = (live > s).astype(jnp.int32)
            if ours:
                use = mine * alive
                at = use * (rel - blocks) + (1 - use) * blocks
                parts.append(own_split[lax.max(lax.min(at, blocks), 0)])
            else:
                use = (1 - mine) * alive
                at = use * (rel - blocks * after_own) + (1 - use) * (2 * blocks)
                parts.append(halo_split[lax.max(lax.min(at, 2 * blocks), 0)])
        return jnp.concatenate(parts, axis=0)

    def times(a, b):
        p = jnp.dot(a, b, preferred_element_type=F32)
        return (p[:tile, :width] + p[tile:, width:]) + (p[:tile, width:] + p[tile:, :width])

    def own_products(i):
        k = lax.rem(i, 2)
        fetch(i).wait()

        @pl.when(i + 1 < chunks)
        def _():
            fetch(i + 1).start()

        for j in range(group):
            row = i * group + j
            hi, lo = split2(jnp.concatenate([stage[k, j, s] for s in range(slots)], axis=1))
            a = jnp.concatenate([hi, lo], axis=0)
            a_split[row] = a
            out[row] = times(a, picked(row, True))

    @pl.loop(0, chunks + 2 * lag)
    def _(i):
        @pl.when(i < chunks)
        def _():
            near_in(i).wait_recv()

            @pl.when(can_fwd)
            def _():
                far(i).start()

            for d in range(1, n_cols):
                sib(i, 0, d).start()

            @pl.when(i + ahead < chunks)
            def _():
                near(i + ahead).start()

            split_halo(near_slot, i, c)

        @pl.when((i >= lag) & (i < chunks + lag) & has_far)
        def _():
            far(i - lag).wait_recv()
            for d in range(1, n_cols):
                sib(i - lag, 1, d).start()
            split_halo(far_slot, i - lag, c)

        @pl.when((i >= lag) & (i < chunks + lag))
        def _():
            for d in range(1, n_cols):
                sib(i - lag, 0, d, True).wait_recv()
                split_halo(near_slot, i - lag, lax.rem(c + n_cols - d, n_cols))

        @pl.when((i >= 2 * lag) & has_far)
        def _():
            for d in range(1, n_cols):
                sib(i - 2 * lag, 1, d, True).wait_recv()
                split_halo(far_slot, i - 2 * lag, lax.rem(c + n_cols - d, n_cols))

        @pl.when(i < chunks)
        def _():
            own_products(i)

    piece_blocks = part_blocks // pieces
    unroll = math.gcd(8, piece_blocks)

    def multiply_piece(col, i):
        first = col * part_blocks + i * piece_blocks

        @pl.loop(0, piece_blocks // unroll)
        def _(j):
            for u in range(unroll):
                row = first + j * unroll + u
                out[row] = out[row] + times(a_split[row], picked(row, False))

    def piece_span(col, i):
        return pl.ds(col * part_blocks + i * piece_blocks, piece_blocks)

    def give(i, d):
        k = (d - 1) * pieces + i
        return remote(out.at[piece_span(lax.rem(c + d, n_cols), i)], got.at[d - 1, piece_span(0, i)],
                      part_s.at[k], part_r.at[k], siblings[d - 1])

    def keep(i):
        return pltpu.make_async_copy(out.at[piece_span(c, i)], rows_out.at[piece_span(0, i)], rows_sem.at[i])

    for d in range(1, n_cols):
        @pl.loop(0, pieces)
        def _(i, d=d):
            multiply_piece(lax.rem(c + d, n_cols), i)
            give(i, d).start()

    gram[...] = jnp.zeros_like(gram)

    @pl.loop(0, pieces)
    def _(i):
        multiply_piece(c, i)
        x = out[piece_span(c, i)]
        for d in range(1, n_cols):
            give(i, d).wait_recv()
            x = x + got[d - 1, piece_span(0, i)]
        out[piece_span(c, i)] = x
        keep(i).start()
        hi, lo = split2(x.reshape(piece_blocks * tile, width))
        gram[...] += lax.dot_general(hi, jnp.concatenate([hi, lo], axis=1), (((0,), (0,)), ((), ())),
                                     preferred_element_type=F32)

    cross = gram[:, width:]
    gram[:, :width] = gram[:, :width] + (cross + cross.T)

    half = width // n_cols

    def half_span(col):
        return pl.ds(pl.multiple_of(col * half, half), half)

    def give_half(d):
        return remote(gram.at[half_span(lax.rem(c + d, n_cols)), pl.ds(0, width)], halves.at[d - 1],
                      half_s.at[d - 1], half_r.at[d - 1], siblings[d - 1])

    for d in range(1, n_cols):
        give_half(d).start()
    total = gram[half_span(c), pl.ds(0, width)]
    for d in range(1, n_cols):
        give_half(d).wait_recv()
        total = total + halves[d - 1]
    acc[0] = total

    def add_up(s):
        return remote(acc.at[s], into.at[s], sum_s.at[s], sum_r.at[s], sum_peers[s])

    n_sums = len(sum_peers)
    for s in range(n_sums):
        add_up(s).start()
        add_up(s).wait_recv()
        acc[s + 1] = acc[s] + into[s]

    def hand_out(d):
        return remote(acc.at[n_sums], full.at[half_span(c)], full_s.at[d - 1], full_r.at[d - 1], siblings[d - 1])

    def hand_in(d):
        return remote(acc.at[n_sums], full.at[half_span(lax.rem(c + n_cols - d, n_cols))],
                      full_s.at[d - 1], full_r.at[d - 1], siblings[d - 1])

    for d in range(1, n_cols):
        hand_out(d).start()

    all_sent(near_s, (partner, c))

    @pl.when(can_fwd)
    def _():
        all_sent(far_s, (fwd_to, c))

    for d in range(1, n_cols):
        all_sent(sib_s.at[d - 1], siblings[d - 1])

        @pl.when(has_far)
        def _(d=d):
            all_sent(sib_s.at[n_cols - 1 + d - 1], siblings[d - 1])

        give_half(d).wait_send()
        for i in range(pieces):
            give(i, d).wait_send()
    for s in range(n_sums):
        add_up(s).wait_send()
    for i in range(pieces):
        keep(i).wait()
    full[half_span(c), :] = acc[n_sums]
    for d in range(1, n_cols):
        hand_in(d).wait_recv()
        hand_out(d).wait_send()
    gram_out[...] = full[...]


def rows_and_gram(tile_cols, live_counts, block_vector, op_tiles, n_rows, n_cols):
    rows, width = block_vector.shape
    blocks, slots, tile, _ = op_tiles.shape
    part = rows // n_cols
    chunks = min(32, blocks)
    while part // chunks > tile:
        chunks *= 2
    pieces = 4
    sums = int(math.log2(n_rows))
    others = max(1, n_cols - 1)
    dma = pltpu.SemaphoreType.DMA
    vmem = pl.BlockSpec(memory_space=pltpu.VMEM)
    smem = pl.BlockSpec(memory_space=pltpu.SMEM)
    hbm = pl.BlockSpec(memory_space=pl.ANY)
    return pl.pallas_call(
        functools.partial(step_kernel, n_rows, n_cols, chunks, 8, 2, pieces),
        out_shape=(
            jax.ShapeDtypeStruct((part // tile, tile, width), F32),
            jax.ShapeDtypeStruct((width, width), F32),
        ),
        in_specs=[smem, smem, hbm, hbm],
        out_specs=(hbm, vmem),
        scratch_shapes=[
            pltpu.VMEM((blocks + 1, tile, 2 * width), BF16),
            pltpu.VMEM((2 * blocks, tile, width), F32),
            pltpu.VMEM((2 * blocks + 1, tile, 2 * width), BF16),
            pltpu.VMEM((2, blocks // chunks, slots, tile, tile), F32),
            pltpu.VMEM((blocks, 2 * tile, slots * tile), BF16),
            pltpu.VMEM((blocks, tile, width), F32),
            pltpu.VMEM((others, part // tile, tile, width), F32),
            pltpu.VMEM((width, 2 * width), F32),
            pltpu.VMEM((others, width // n_cols, width), F32),
            pltpu.VMEM((sums + 1, width // n_cols, width), F32),
            pltpu.VMEM((sums, width // n_cols, width), F32),
            pltpu.VMEM((width, width), F32),
            dma, dma((2,)), dma((pieces,)),
            dma, dma((chunks,)), dma, dma((chunks,)), dma((2 * others,)), dma((2 * others * chunks,)),
            dma((others * pieces,)), dma((others * pieces,)),
            dma((others,)), dma((others,)), dma((sums,)), dma((sums,)), dma((others,)), dma((others,)),
        ],
        compiler_params=pltpu.CompilerParams(collective_id=0, has_side_effects=True, vmem_limit_bytes=48 * MIB),
        name="rows_and_gram",
    )(tile_cols.T, live_counts, block_vector.reshape(blocks, tile, width), op_tiles)


def spread(x):
    x1 = x.astype(BF16).astype(F32)
    x2 = (x - x1).astype(BF16).astype(F32)
    return x1, x2, x - x1 - x2


def factor(gram):
    n = gram.shape[0]
    nb = PANEL
    lane = lax.broadcasted_iota(jnp.int32, (nb, n), 1)
    sub = lax.broadcasted_iota(jnp.int32, (nb, n), 0)
    eye = (lax.broadcasted_iota(jnp.int32, (n, n), 0) == lax.broadcasted_iota(jnp.int32, (n, n), 1)).astype(F32)
    left, right = gram, eye
    upper, inverse = [], []
    for p in range(n // nb):
        a = left[:nb]
        w = right[:nb]
        cols = [jnp.broadcast_to(a[:, p * nb + k:p * nb + k + 1], (nb, n)) for k in range(nb)]
        for j in range(nb):
            scale = lax.rsqrt(jnp.broadcast_to(cols[j][j:j + 1], (nb, n)))
            col = cols[j] * scale
            below = jnp.where(sub > j, col, 0.0)
            for k in range(j + 1, nb):
                cols[k] = cols[k] - below * jnp.broadcast_to(col[k:k + 1], (nb, n))
            a_row = jnp.broadcast_to(a[j:j + 1], (nb, n)) * scale
            w_row = jnp.broadcast_to(w[j:j + 1], (nb, n)) * scale
            a = jnp.where(sub == j, a_row, a - below * a_row)
            w = jnp.where(sub == j, w_row, w - below * w_row)
        upper.append(jnp.where(lane >= sub + p * nb, a, 0.0))
        inverse.append(w)
        rest = n - (p + 1) * nb
        if rest:
            a1, a2, a3 = spread(a)
            w1, w2, w3 = spread(w)
            lhs = jnp.concatenate([a1, a1, a2, a1, a2, a3], axis=0).T[n - rest:].astype(BF16)
            rhs_a = jnp.concatenate([a1, a2, a1, a3, a2, a1], axis=0)
            rhs_w = jnp.concatenate([w1, w2, w1, w3, w2, w1], axis=0)
            rhs = jnp.concatenate([rhs_a, rhs_w], axis=1).astype(BF16)
            change = jnp.dot(lhs, rhs, preferred_element_type=F32)
            left = left[nb:] - change[:, :n]
            right = right[nb:] - change[:, n:]
    return jnp.concatenate(upper, axis=0), jnp.concatenate(inverse, axis=0)


def basis_kernel(root, gram, rows, basis, r_factor, solve):
    @pl.when(pl.program_id(0) == 0)
    def _():
        upper, inverse = factor(gram[...])
        r_factor[...] = upper / root
        solve[...] = inverse * root

    width = rows.shape[1]
    x_hi, x_lo = split2(rows[...])
    s_hi, s_lo = split2(solve[...])
    both = lax.dot_general(x_hi, jnp.concatenate([s_hi, s_lo], axis=0), (((1,), (1,)), ((), ())),
                           preferred_element_type=F32)
    rest = lax.dot_general(x_lo, s_hi, (((1,), (1,)), ((), ())), preferred_element_type=F32)
    basis[...] = both[:, :width] + both[:, width:] + rest


def basis_of(gram, rows, root):
    part, width = rows.shape
    size = min(part, 1024)
    return pl.pallas_call(
        functools.partial(basis_kernel, root),
        out_shape=(jax.ShapeDtypeStruct((part, width), F32), jax.ShapeDtypeStruct((width, width), F32)),
        grid=(part // size,),
        in_specs=[
            pl.BlockSpec((width, width), lambda i: (0, 0)),
            pl.BlockSpec((size, width), lambda i: (i, 0)),
        ],
        out_specs=(
            pl.BlockSpec((size, width), lambda i: (i, 0)),
            pl.BlockSpec((width, width), lambda i: (0, 0)),
        ),
        scratch_shapes=[pltpu.VMEM((width, width), F32)],
        compiler_params=pltpu.CompilerParams(vmem_limit_bytes=24 * MIB),
        name="factor_and_basis",
    )(gram, rows)


def on_device(n_rows, n_cols, block_vector, op_tiles, tile_cols, live_counts):
    rows, gram = rows_and_gram(tile_cols, live_counts, block_vector, op_tiles, n_rows, n_cols)
    root = math.sqrt(block_vector.shape[0] * n_rows)
    return basis_of(gram, rows.reshape(-1, rows.shape[2]), root)


def solution(mesh):
    in_specs = (P("rows", None), P("rows", "cols", None, None), P("rows", "cols"), P("rows"))
    out_specs = (P(("rows", "cols"), None), P())
    return jax.shard_map(
        functools.partial(on_device, mesh.shape["rows"], mesh.shape["cols"]),
        mesh=mesh, in_specs=in_specs, out_specs=out_specs, check_vma=False,
    )
```

```python
import functools
import math

import jax
import jax.numpy as jnp
from jax import lax
from jax.experimental import pallas as pl
from jax.experimental.pallas import tpu as pltpu
from jax.sharding import PartitionSpec as P

MESH = pl.DeviceIdType.MESH
BF16 = jnp.bfloat16
F32 = jnp.float32
MIB = 1024 * 1024
PANEL = 16


def split2(x):
    hi = x.astype(BF16)
    lo = (x - hi.astype(F32)).astype(BF16)
    return hi, lo


def greet(peers):
    barrier = pltpu.get_barrier_semaphore()
    for cond, device in peers:
        if cond is None:
            pl.semaphore_signal(barrier, inc=1, device_id=device, device_id_type=MESH)
        else:
            @pl.when(cond)
            def _(device=device):
                pl.semaphore_signal(barrier, inc=1, device_id=device, device_id_type=MESH)
    total = 0
    for cond, _ in peers:
        total = total + (1 if cond is None else jnp.where(cond, 1, 0))
    pl.semaphore_wait(barrier, total)


def rounds_of(n_rows):
    rounds = []
    stride = 1
    while stride < n_rows:
        radix = min(4, n_rows // stride)
        rounds.append((stride, radix))
        stride *= radix
    return rounds


def packed_rows(width, n_cols):
    packed = width * 3 // 4
    return packed if width == 128 and packed % (8 * n_cols) == 0 else width


def pack(gram, rows):
    n = gram.shape[0]
    if rows == n:
        return gram
    h, q = n // 2, n // 4
    lane = lax.broadcasted_iota(jnp.int32, (q, n), 1)
    folded = jnp.where(lane < h, pltpu.roll(gram[h:h + q], h, axis=1), gram[h + q:])
    return jnp.concatenate([gram[:h], folded], axis=0)


def unpack(packed, n):
    if packed.shape[0] == n:
        return packed
    folded = packed[n // 2:]
    return jnp.concatenate([packed[:n // 2], pltpu.roll(folded, n // 2, axis=1), folded], axis=0)


def step_kernel(n_rows, n_cols, chunks, ahead, lag, pieces, cols_in, counts_in, own, tiles, rows_out, gram_out,
                cols, counts, own_split, halo, halo_split, stage, a_split, out, got, gram, sent, halves, acc, into, full,
                small_sem, own_sem, stage_sem, rows_sem, near_s, near_r, far_s, far_r, sib_s, sib_r, part_s, part_r,
                half_s, half_r, sum_s, sum_r, full_s, full_r):
    r = lax.axis_index("rows")
    c = lax.axis_index("cols")
    blocks, slots, tile, _ = tiles.shape
    rows, width = blocks * tile, own.shape[2]
    odd = lax.rem(r, 2)
    partner = r + 1 - 2 * odd
    fwd_to = r + 2 - 4 * odd
    far_from = r - 2 + 4 * odd
    can_fwd = (fwd_to >= 0) & (fwd_to < n_rows)
    has_far = (far_from >= 0) & (far_from < n_rows)
    part = rows // n_cols
    part_blocks = part // tile
    size = part // chunks
    near_slot = 1 - odd
    far_slot = odd
    siblings = [(r, lax.rem(c + d, n_cols)) for d in range(1, n_cols)]
    sum_rounds = []
    for first, radix in rounds_of(n_rows):
        digit = lax.rem(r // first, radix)
        low, high = lax.rem(digit, 2), digit // 2
        others = []
        for k in range(1, radix):
            new_low = 1 - low if k % 2 else low
            new_high = 1 - high if k // 2 else high
            others.append((r + (new_low - low + 2 * (new_high - high)) * first, c))
        sum_rounds.append(others)

    peers = [(None, (partner, c)), (can_fwd, (fwd_to, c)), (has_far, (far_from, c))]
    peers += [(None, device) for device in siblings]
    peers += [(None, device) for others in sum_rounds for device in others if device is not sum_rounds[0][0]]

    def remote(src, dst, send_sem, recv_sem, device):
        return pltpu.make_async_remote_copy(
            src_ref=src, dst_ref=dst, send_sem=send_sem, recv_sem=recv_sem, device_id=device, device_id_type=MESH)

    def chunk_place(i, col):
        row = col * part + i * size
        return row // tile, pl.ds(pl.multiple_of(lax.rem(row, tile), size), size)

    def own_at(i, col):
        block, span = chunk_place(i, col)
        return own.at[block, span]

    def halo_at(slot, i, col):
        block, span = chunk_place(i, col)
        return halo.at[slot * blocks + block, span]

    def near(i):
        return remote(own_at(i, c), halo_at(odd, i, c), near_s, near_r.at[i], (partner, c))

    def near_in(i):
        return remote(own_at(i, c), halo_at(near_slot, i, c), near_s, near_r.at[i], (partner, c))

    def far(i):
        return remote(halo_at(near_slot, i, c), halo_at(far_slot, i, c), far_s, far_r.at[i], (fwd_to, c))

    def sib(i, kind, d, incoming=False):
        slot = near_slot if kind == 0 else far_slot
        k = (kind * (n_cols - 1) + d - 1) * chunks + i
        col = lax.rem(c + n_cols - d, n_cols) if incoming else c
        return remote(halo_at(slot, i, c), halo_at(slot, i, col),
                      sib_s.at[kind * (n_cols - 1) + d - 1], sib_r.at[k], siblings[d - 1])

    def all_sent(sem, device):
        whole = halo.at[pl.ds(near_slot * blocks + c * part_blocks, part_blocks)]
        remote(whole, whole, sem, near_r.at[0], device).wait_send()

    group = blocks // chunks

    def fetch(i):
        k = lax.rem(i, 2)
        return pltpu.make_async_copy(tiles.at[pl.ds(i * group, group)], stage.at[k], stage_sem.at[k])

    bring_cols = pltpu.make_async_copy(cols_in, cols, small_sem.at[0])
    bring_counts = pltpu.make_async_copy(counts_in, counts, small_sem.at[1])
    bring_cols.start()
    bring_counts.start()
    bring_own = pltpu.make_async_copy(own, out, own_sem)
    bring_own.start()
    fetch(0).start()
    greet(peers)
    for i in range(ahead):
        near(i).start()

    def split_halo(slot, i, col):
        block, span = chunk_place(i, col)
        hi, lo = split2(halo[slot * blocks + block, span, :])
        halo_split[slot * blocks + block, span, :] = jnp.concatenate([hi, lo], axis=1)

    own_split[blocks] = jnp.zeros((tile, 2 * width), BF16)
    halo_split[2 * blocks] = jnp.zeros((tile, 2 * width), BF16)
    bring_cols.wait()
    bring_counts.wait()
    bring_own.wait()

    @pl.loop(0, blocks)
    def _(i):
        hi, lo = split2(out[i])
        own_split[i] = jnp.concatenate([hi, lo], axis=1)

    before = (r - 1) * blocks
    first_slot = c * slots

    def picked(row, ours):
        live = counts[row] - first_slot
        parts = []
        for s in range(slots):
            rel = cols[s, row] - before
            after_prev = (rel >= blocks).astype(jnp.int32)
            after_own = (rel >= 2 * blocks).astype(jnp.int32)
            mine = after_prev - after_own
            alive = (live > s).astype(jnp.int32)
            if ours:
                use = mine * alive
                at = use * (rel - blocks) + (1 - use) * blocks
                parts.append(own_split[lax.max(lax.min(at, blocks), 0)])
            else:
                use = (1 - mine) * alive
                at = use * (rel - blocks * after_own) + (1 - use) * (2 * blocks)
                parts.append(halo_split[lax.max(lax.min(at, 2 * blocks), 0)])
        return jnp.concatenate(parts, axis=0)

    def times(a, b):
        p = jnp.dot(a, b, preferred_element_type=F32)
        return (p[:tile, :width] + p[tile:, width:]) + (p[:tile, width:] + p[tile:, :width])

    def own_products(i):
        k = lax.rem(i, 2)
        fetch(i).wait()

        @pl.when(i + 1 < chunks)
        def _():
            fetch(i + 1).start()

        for j in range(group):
            row = i * group + j
            hi, lo = split2(jnp.concatenate([stage[k, j, s] for s in range(slots)], axis=1))
            a = jnp.concatenate([hi, lo], axis=0)
            a_split[row] = a
            out[row] = times(a, picked(row, True))

    @pl.loop(0, chunks + 2 * lag)
    def _(i):
        @pl.when(i < chunks)
        def _():
            near_in(i).wait_recv()

            @pl.when(can_fwd)
            def _():
                far(i).start()

            for d in range(1, n_cols):
                sib(i, 0, d).start()

            @pl.when(i + ahead < chunks)
            def _():
                near(i + ahead).start()

            split_halo(near_slot, i, c)

        @pl.when((i >= lag) & (i < chunks + lag) & has_far)
        def _():
            far(i - lag).wait_recv()
            for d in range(1, n_cols):
                sib(i - lag, 1, d).start()
            split_halo(far_slot, i - lag, c)

        @pl.when((i >= lag) & (i < chunks + lag))
        def _():
            for d in range(1, n_cols):
                sib(i - lag, 0, d, True).wait_recv()
                split_halo(near_slot, i - lag, lax.rem(c + n_cols - d, n_cols))

        @pl.when((i >= 2 * lag) & has_far)
        def _():
            for d in range(1, n_cols):
                sib(i - 2 * lag, 1, d, True).wait_recv()
                split_halo(far_slot, i - 2 * lag, lax.rem(c + n_cols - d, n_cols))

        @pl.when(i < chunks)
        def _():
            own_products(i)

    piece_blocks = part_blocks // pieces
    unroll = math.gcd(8, piece_blocks)

    def multiply_piece(col, i):
        first = col * part_blocks + i * piece_blocks

        @pl.loop(0, piece_blocks // unroll)
        def _(j):
            for u in range(unroll):
                row = first + j * unroll + u
                out[row] = out[row] + times(a_split[row], picked(row, False))

    def piece_span(col, i):
        return pl.ds(col * part_blocks + i * piece_blocks, piece_blocks)

    def give(i, d):
        k = (d - 1) * pieces + i
        return remote(out.at[piece_span(lax.rem(c + d, n_cols), i)], got.at[d - 1, piece_span(0, i)],
                      part_s.at[k], part_r.at[k], siblings[d - 1])

    def keep(i):
        return pltpu.make_async_copy(out.at[piece_span(c, i)], rows_out.at[piece_span(0, i)], rows_sem.at[i])

    for d in range(1, n_cols):
        @pl.loop(0, pieces)
        def _(i, d=d):
            multiply_piece(lax.rem(c + d, n_cols), i)
            give(i, d).start()

    gram[...] = jnp.zeros_like(gram)

    @pl.loop(0, pieces)
    def _(i):
        multiply_piece(c, i)
        x = out[piece_span(c, i)]
        for d in range(1, n_cols):
            give(i, d).wait_recv()
            x = x + got[d - 1, piece_span(0, i)]
        out[piece_span(c, i)] = x
        keep(i).start()
        hi, lo = split2(x.reshape(piece_blocks * tile, width))
        gram[...] += lax.dot_general(hi, jnp.concatenate([hi, lo], axis=1), (((0,), (0,)), ((), ())),
                                     preferred_element_type=F32)

    cross = gram[:, width:]
    sent[...] = pack(gram[:, :width] + (cross + cross.T), sent.shape[0])

    half = sent.shape[0] // n_cols

    def half_span(col):
        return pl.ds(pl.multiple_of(col * half, half), half)

    def give_half(d):
        return remote(sent.at[half_span(lax.rem(c + d, n_cols))], halves.at[d - 1],
                      half_s.at[d - 1], half_r.at[d - 1], siblings[d - 1])

    for d in range(1, n_cols):
        give_half(d).start()
    total = sent[half_span(c), :]
    for d in range(1, n_cols):
        give_half(d).wait_recv()
        total = total + halves[d - 1]
    acc[0] = total

    def add_up(s, k):
        at = 3 * s + k
        return remote(acc.at[s], into.at[at], sum_s.at[at], sum_r.at[at], sum_rounds[s][k])

    n_sums = len(sum_rounds)
    for s in range(n_sums):
        n_others = len(sum_rounds[s])
        for k in range(n_others):
            add_up(s, k).start()
        for k in range(n_others):
            add_up(s, k).wait_recv()
        total = acc[s] + into[3 * s]
        if n_others == 3:
            total = total + (into[3 * s + 1] + into[3 * s + 2])
        acc[s + 1] = total

    def hand_out(d):
        return remote(acc.at[n_sums], full.at[half_span(c)], full_s.at[d - 1], full_r.at[d - 1], siblings[d - 1])

    def hand_in(d):
        return remote(acc.at[n_sums], full.at[half_span(lax.rem(c + n_cols - d, n_cols))],
                      full_s.at[d - 1], full_r.at[d - 1], siblings[d - 1])

    for d in range(1, n_cols):
        hand_out(d).start()

    all_sent(near_s, (partner, c))

    @pl.when(can_fwd)
    def _():
        all_sent(far_s, (fwd_to, c))

    for d in range(1, n_cols):
        all_sent(sib_s.at[d - 1], siblings[d - 1])

        @pl.when(has_far)
        def _(d=d):
            all_sent(sib_s.at[n_cols - 1 + d - 1], siblings[d - 1])

        give_half(d).wait_send()
        for i in range(pieces):
            give(i, d).wait_send()
    for s in range(n_sums):
        for k in range(len(sum_rounds[s])):
            add_up(s, k).wait_send()
    for i in range(pieces):
        keep(i).wait()
    full[half_span(c), :] = acc[n_sums]
    for d in range(1, n_cols):
        hand_in(d).wait_recv()
        hand_out(d).wait_send()
    gram_out[...] = unpack(full[...], width)


def rows_and_gram(tile_cols, live_counts, block_vector, op_tiles, n_rows, n_cols):
    rows, width = block_vector.shape
    blocks, slots, tile, _ = op_tiles.shape
    part = rows // n_cols
    chunks = min(32, blocks)
    while part // chunks > tile:
        chunks *= 2
    pieces = 4
    sums = len(rounds_of(n_rows))
    others = max(1, n_cols - 1)
    packed = packed_rows(width, n_cols)
    half = packed // n_cols
    dma = pltpu.SemaphoreType.DMA
    vmem = pl.BlockSpec(memory_space=pltpu.VMEM)
    small = pl.BlockSpec(memory_space=pltpu.HBM)
    hbm = pl.BlockSpec(memory_space=pl.ANY)
    return pl.pallas_call(
        functools.partial(step_kernel, n_rows, n_cols, chunks, 8, 2, pieces),
        out_shape=(
            jax.ShapeDtypeStruct((part // tile, tile, width), F32),
            jax.ShapeDtypeStruct((width, width), F32),
        ),
        in_specs=[small, small, hbm, hbm],
        out_specs=(hbm, vmem),
        scratch_shapes=[
            pltpu.SMEM((slots, blocks), jnp.int32),
            pltpu.SMEM((blocks,), jnp.int32),
            pltpu.VMEM((blocks + 1, tile, 2 * width), BF16),
            pltpu.VMEM((2 * blocks, tile, width), F32),
            pltpu.VMEM((2 * blocks + 1, tile, 2 * width), BF16),
            pltpu.VMEM((2, blocks // chunks, slots, tile, tile), F32),
            pltpu.VMEM((blocks, 2 * tile, slots * tile), BF16),
            pltpu.VMEM((blocks, tile, width), F32),
            pltpu.VMEM((others, part // tile, tile, width), F32),
            pltpu.VMEM((width, 2 * width), F32),
            pltpu.VMEM((packed, width), F32),
            pltpu.VMEM((others, half, width), F32),
            pltpu.VMEM((sums + 1, half, width), F32),
            pltpu.VMEM((3 * sums, half, width), F32),
            pltpu.VMEM((packed, width), F32),
            dma((2,)), dma, dma((2,)), dma((pieces,)),
            dma, dma((chunks,)), dma, dma((chunks,)), dma((2 * others,)), dma((2 * others * chunks,)),
            dma((others * pieces,)), dma((others * pieces,)),
            dma((others,)), dma((others,)), dma((3 * sums,)), dma((3 * sums,)), dma((others,)), dma((others,)),
        ],
        compiler_params=pltpu.CompilerParams(collective_id=0, has_side_effects=True, vmem_limit_bytes=48 * MIB),
        name="rows_and_gram",
    )(tile_cols.T, live_counts, block_vector.reshape(blocks, tile, width), op_tiles)


def spread(x):
    x1 = x.astype(BF16).astype(F32)
    x2 = (x - x1).astype(BF16).astype(F32)
    return x1, x2, x - x1 - x2


def factor(gram):
    n = gram.shape[0]
    nb = PANEL
    lane = lax.broadcasted_iota(jnp.int32, (nb, n), 1)
    sub = lax.broadcasted_iota(jnp.int32, (nb, n), 0)
    eye = (lax.broadcasted_iota(jnp.int32, (n, n), 0) == lax.broadcasted_iota(jnp.int32, (n, n), 1)).astype(F32)
    left, right = gram, eye
    upper, inverse = [], []
    for p in range(n // nb):
        a = left[:nb]
        w = right[:nb]
        cols = [jnp.broadcast_to(a[:, p * nb + k:p * nb + k + 1], (nb, n)) for k in range(nb)]
        for j in range(nb):
            scale = lax.rsqrt(jnp.broadcast_to(cols[j][j:j + 1], (nb, n)))
            col = cols[j] * scale
            below = jnp.where(sub > j, col, 0.0)
            for k in range(j + 1, nb):
                cols[k] = cols[k] - below * jnp.broadcast_to(col[k:k + 1], (nb, n))
            a_row = jnp.broadcast_to(a[j:j + 1], (nb, n)) * scale
            w_row = jnp.broadcast_to(w[j:j + 1], (nb, n)) * scale
            a = jnp.where(sub == j, a_row, a - below * a_row)
            w = jnp.where(sub == j, w_row, w - below * w_row)
        upper.append(jnp.where(lane >= sub + p * nb, a, 0.0))
        inverse.append(w)
        rest = n - (p + 1) * nb
        if rest:
            a1, a2, a3 = spread(a)
            w1, w2, w3 = spread(w)
            lhs = jnp.concatenate([a1, a1, a2, a1, a2, a3], axis=0).T[n - rest:].astype(BF16)
            rhs_a = jnp.concatenate([a1, a2, a1, a3, a2, a1], axis=0)
            rhs_w = jnp.concatenate([w1, w2, w1, w3, w2, w1], axis=0)
            rhs = jnp.concatenate([rhs_a, rhs_w], axis=1).astype(BF16)
            change = jnp.dot(lhs, rhs, preferred_element_type=F32)
            left = left[nb:] - change[:, :n]
            right = right[nb:] - change[:, n:]
    return jnp.concatenate(upper, axis=0), jnp.concatenate(inverse, axis=0)


def basis_kernel(root, gram, rows, basis, r_factor, solve):
    @pl.when(pl.program_id(0) == 0)
    def _():
        upper, inverse = factor(gram[...])
        r_factor[...] = upper / root
        solve[...] = inverse * root

    width = rows.shape[1]
    x_hi, x_lo = split2(rows[...])
    s_hi, s_lo = split2(solve[...])
    both = lax.dot_general(x_hi, jnp.concatenate([s_hi, s_lo], axis=0), (((1,), (1,)), ((), ())),
                           preferred_element_type=F32)
    rest = lax.dot_general(x_lo, s_hi, (((1,), (1,)), ((), ())), preferred_element_type=F32)
    basis[...] = both[:, :width] + both[:, width:] + rest


def basis_of(gram, rows, root):
    part, width = rows.shape
    size = min(part, 1024)
    return pl.pallas_call(
        functools.partial(basis_kernel, root),
        out_shape=(jax.ShapeDtypeStruct((part, width), F32), jax.ShapeDtypeStruct((width, width), F32)),
        grid=(part // size,),
        in_specs=[
            pl.BlockSpec((width, width), lambda i: (0, 0)),
            pl.BlockSpec((size, width), lambda i: (i, 0)),
        ],
        out_specs=(
            pl.BlockSpec((size, width), lambda i: (i, 0)),
            pl.BlockSpec((width, width), lambda i: (0, 0)),
        ),
        scratch_shapes=[pltpu.VMEM((width, width), F32)],
        compiler_params=pltpu.CompilerParams(vmem_limit_bytes=24 * MIB),
        name="factor_and_basis",
    )(gram, rows)


def on_device(n_rows, n_cols, block_vector, op_tiles, tile_cols, live_counts):
    rows, gram = rows_and_gram(tile_cols, live_counts, block_vector, op_tiles, n_rows, n_cols)
    root = math.sqrt(block_vector.shape[0] * n_rows)
    return basis_of(gram, rows.reshape(-1, rows.shape[2]), root)


def solution(mesh):
    in_specs = (P("rows", None), P("rows", "cols", None, None), P("rows", "cols"), P("rows"))
    out_specs = (P(("rows", "cols"), None), P())
    return jax.shard_map(
        functools.partial(on_device, mesh.shape["rows"], mesh.shape["cols"]),
        mesh=mesh, in_specs=in_specs, out_specs=out_specs, check_vma=False,
    )
```

```python
import functools
import math

import jax
import jax.numpy as jnp
from jax import lax
from jax.experimental import pallas as pl
from jax.experimental.pallas import tpu as pltpu
from jax.sharding import PartitionSpec as P

MESH = pl.DeviceIdType.MESH
BF16 = jnp.bfloat16
F32 = jnp.float32
MIB = 1024 * 1024
PANEL = 16


def split2(x):
    hi = x.astype(BF16)
    lo = (x - hi.astype(F32)).astype(BF16)
    return hi, lo


def greet(peers):
    barrier = pltpu.get_barrier_semaphore()
    for cond, device in peers:
        if cond is None:
            pl.semaphore_signal(barrier, inc=1, device_id=device, device_id_type=MESH)
        else:
            @pl.when(cond)
            def _(device=device):
                pl.semaphore_signal(barrier, inc=1, device_id=device, device_id_type=MESH)
    total = 0
    for cond, _ in peers:
        total = total + (1 if cond is None else jnp.where(cond, 1, 0))
    pl.semaphore_wait(barrier, total)


def rounds_of(n_rows):
    rounds = []
    stride = 1
    while stride < n_rows:
        radix = min(4, n_rows // stride)
        rounds.append((stride, radix))
        stride *= radix
    return rounds


def packed_rows(width, n_cols):
    packed = width * 3 // 4
    return packed if width == 128 and packed % (8 * n_cols) == 0 else width


def pack(gram, rows):
    n = gram.shape[0]
    if rows == n:
        return gram
    h, q = n // 2, n // 4
    lane = lax.broadcasted_iota(jnp.int32, (q, n), 1)
    folded = jnp.where(lane < h, pltpu.roll(gram[h:h + q], h, axis=1), gram[h + q:])
    return jnp.concatenate([gram[:h], folded], axis=0)


def unpack(packed, n):
    if packed.shape[0] == n:
        return packed
    folded = packed[n // 2:]
    return jnp.concatenate([packed[:n // 2], pltpu.roll(folded, n // 2, axis=1), folded], axis=0)


def step_kernel(n_rows, n_cols, chunks, ahead, lag, pieces, cols_in, counts_in, own, tiles, rows_out, gram_out,
                cols, counts, own_split, halo, halo_split, stage, a_split, out, got, gram, sent, halves, acc, into, full,
                small_sem, own_sem, stage_sem, rows_sem, near_s, near_r, far_s, far_r, sib_s, sib_r, part_s, part_r,
                half_s, half_r, sum_s, sum_r, full_s, full_r):
    r = lax.axis_index("rows")
    c = lax.axis_index("cols")
    blocks, slots, tile, _ = tiles.shape
    rows, width = blocks * tile, own.shape[2]
    odd = lax.rem(r, 2)
    partner = r + 1 - 2 * odd
    fwd_to = r + 2 - 4 * odd
    far_from = r - 2 + 4 * odd
    can_fwd = (fwd_to >= 0) & (fwd_to < n_rows)
    has_far = (far_from >= 0) & (far_from < n_rows)
    part = rows // n_cols
    part_blocks = part // tile
    size = part // chunks
    near_slot = 1 - odd
    far_slot = odd
    siblings = [(r, lax.rem(c + d, n_cols)) for d in range(1, n_cols)]
    sum_rounds = []
    for first, radix in rounds_of(n_rows):
        digit = lax.rem(r // first, radix)
        low, high = lax.rem(digit, 2), digit // 2
        others = []
        for k in range(1, radix):
            new_low = 1 - low if k % 2 else low
            new_high = 1 - high if k // 2 else high
            others.append((r + (new_low - low + 2 * (new_high - high)) * first, c))
        sum_rounds.append(others)

    peers = [(None, (partner, c)), (can_fwd, (fwd_to, c)), (has_far, (far_from, c))]
    peers += [(None, device) for device in siblings]
    peers += [(None, device) for others in sum_rounds for device in others if device is not sum_rounds[0][0]]

    def remote(src, dst, send_sem, recv_sem, device):
        return pltpu.make_async_remote_copy(
            src_ref=src, dst_ref=dst, send_sem=send_sem, recv_sem=recv_sem, device_id=device, device_id_type=MESH)

    def chunk_place(i, col):
        row = col * part + i * size
        return row // tile, pl.ds(pl.multiple_of(lax.rem(row, tile), size), size)

    def own_at(i, col):
        block, span = chunk_place(i, col)
        return own.at[block, span]

    def halo_at(slot, i, col):
        block, span = chunk_place(i, col)
        return halo.at[slot * blocks + block, span]

    def near(i):
        return remote(own_at(i, c), halo_at(odd, i, c), near_s, near_r.at[i], (partner, c))

    def near_in(i):
        return remote(own_at(i, c), halo_at(near_slot, i, c), near_s, near_r.at[i], (partner, c))

    def far(i):
        return remote(halo_at(near_slot, i, c), halo_at(far_slot, i, c), far_s, far_r.at[i], (fwd_to, c))

    def sib(i, kind, d, incoming=False):
        slot = near_slot if kind == 0 else far_slot
        k = (kind * (n_cols - 1) + d - 1) * chunks + i
        col = lax.rem(c + n_cols - d, n_cols) if incoming else c
        return remote(halo_at(slot, i, c), halo_at(slot, i, col),
                      sib_s.at[kind * (n_cols - 1) + d - 1], sib_r.at[k], siblings[d - 1])

    def all_sent(sem, device):
        whole = halo.at[pl.ds(near_slot * blocks + c * part_blocks, part_blocks)]
        remote(whole, whole, sem, near_r.at[0], device).wait_send()

    group = blocks // chunks

    def fetch(i):
        k = lax.rem(i, 2)
        return pltpu.make_async_copy(tiles.at[pl.ds(i * group, group)], stage.at[k], stage_sem.at[k])

    bring_cols = pltpu.make_async_copy(cols_in, cols, small_sem.at[0])
    bring_counts = pltpu.make_async_copy(counts_in, counts, small_sem.at[1])
    bring_cols.start()
    bring_counts.start()
    bring_own = pltpu.make_async_copy(own, out, own_sem)
    bring_own.start()
    fetch(0).start()
    greet(peers)
    for i in range(ahead):
        near(i).start()

    def split_halo(slot, i, col):
        block, span = chunk_place(i, col)
        hi, lo = split2(halo[slot * blocks + block, span, :])
        halo_split[slot * blocks + block, span, :] = jnp.concatenate([hi, lo], axis=1)

    own_split[blocks] = jnp.zeros((tile, 2 * width), BF16)
    halo_split[2 * blocks] = jnp.zeros((tile, 2 * width), BF16)

    split_steps = 2 * lag
    per_step = blocks // split_steps

    def split_own(i):
        @pl.loop(0, per_step)
        def _(j):
            hi, lo = split2(out[i * per_step + j])
            own_split[i * per_step + j] = jnp.concatenate([hi, lo], axis=1)

    before = (r - 1) * blocks
    first_slot = c * slots

    def picked(row, ours):
        live = counts[row] - first_slot
        parts = []
        for s in range(slots):
            rel = cols[s, row] - before
            after_prev = (rel >= blocks).astype(jnp.int32)
            after_own = (rel >= 2 * blocks).astype(jnp.int32)
            mine = after_prev - after_own
            alive = (live > s).astype(jnp.int32)
            if ours:
                use = mine * alive
                at = use * (rel - blocks) + (1 - use) * blocks
                parts.append(own_split[lax.max(lax.min(at, blocks), 0)])
            else:
                use = (1 - mine) * alive
                at = use * (rel - blocks * after_own) + (1 - use) * (2 * blocks)
                parts.append(halo_split[lax.max(lax.min(at, 2 * blocks), 0)])
        return jnp.concatenate(parts, axis=0)

    def times(a, b):
        p = jnp.dot(a, b, preferred_element_type=F32)
        return (p[:tile, :width] + p[tile:, width:]) + (p[:tile, width:] + p[tile:, :width])

    def own_products(i):
        k = lax.rem(i, 2)
        fetch(i).wait()

        @pl.when(i + 1 < chunks)
        def _():
            fetch(i + 1).start()

        for j in range(group):
            row = i * group + j
            hi, lo = split2(jnp.concatenate([stage[k, j, s] for s in range(slots)], axis=1))
            a = jnp.concatenate([hi, lo], axis=0)
            a_split[row] = a
            out[row] = times(a, picked(row, True))

    @pl.loop(0, chunks + 2 * lag)
    def _(i):
        @pl.when(i < chunks)
        def _():
            near_in(i).wait_recv()

            @pl.when(can_fwd)
            def _():
                far(i).start()

            for d in range(1, n_cols):
                sib(i, 0, d).start()

            @pl.when(i + ahead < chunks)
            def _():
                near(i + ahead).start()

            split_halo(near_slot, i, c)

        @pl.when((i >= lag) & (i < chunks + lag) & has_far)
        def _():
            far(i - lag).wait_recv()
            for d in range(1, n_cols):
                sib(i - lag, 1, d).start()
            split_halo(far_slot, i - lag, c)

        @pl.when((i >= lag) & (i < chunks + lag))
        def _():
            for d in range(1, n_cols):
                sib(i - lag, 0, d, True).wait_recv()
                split_halo(near_slot, i - lag, lax.rem(c + n_cols - d, n_cols))

        @pl.when((i >= 2 * lag) & has_far)
        def _():
            for d in range(1, n_cols):
                sib(i - 2 * lag, 1, d, True).wait_recv()
                split_halo(far_slot, i - 2 * lag, lax.rem(c + n_cols - d, n_cols))

        @pl.when(i == 0)
        def _():
            bring_own.wait()
            bring_cols.wait()
            bring_counts.wait()

        @pl.when(i < split_steps)
        def _():
            split_own(i)

        @pl.when(i >= split_steps)
        def _():
            own_products(i - split_steps)

    piece_blocks = part_blocks // pieces
    unroll = math.gcd(8, piece_blocks)

    def multiply_piece(col, i):
        first = col * part_blocks + i * piece_blocks

        @pl.loop(0, piece_blocks // unroll)
        def _(j):
            for u in range(unroll):
                row = first + j * unroll + u
                out[row] = out[row] + times(a_split[row], picked(row, False))

    def piece_span(col, i):
        return pl.ds(col * part_blocks + i * piece_blocks, piece_blocks)

    def give(i, d):
        k = (d - 1) * pieces + i
        return remote(out.at[piece_span(lax.rem(c + d, n_cols), i)], got.at[d - 1, piece_span(0, i)],
                      part_s.at[k], part_r.at[k], siblings[d - 1])

    def keep(i):
        return pltpu.make_async_copy(out.at[piece_span(c, i)], rows_out.at[piece_span(0, i)], rows_sem.at[i])

    for d in range(1, n_cols):
        @pl.loop(0, pieces)
        def _(i, d=d):
            multiply_piece(lax.rem(c + d, n_cols), i)
            give(i, d).start()

    gram[...] = jnp.zeros_like(gram)

    @pl.loop(0, pieces)
    def _(i):
        multiply_piece(c, i)
        x = out[piece_span(c, i)]
        for d in range(1, n_cols):
            give(i, d).wait_recv()
            x = x + got[d - 1, piece_span(0, i)]
        out[piece_span(c, i)] = x
        keep(i).start()
        hi, lo = split2(x.reshape(piece_blocks * tile, width))
        gram[...] += lax.dot_general(hi, jnp.concatenate([hi, lo], axis=1), (((0,), (0,)), ((), ())),
                                     preferred_element_type=F32)

    cross = gram[:, width:]
    sent[...] = pack(gram[:, :width] + (cross + cross.T), sent.shape[0])

    half = sent.shape[0] // n_cols

    def half_span(col):
        return pl.ds(pl.multiple_of(col * half, half), half)

    def give_half(d):
        return remote(sent.at[half_span(lax.rem(c + d, n_cols))], halves.at[d - 1],
                      half_s.at[d - 1], half_r.at[d - 1], siblings[d - 1])

    for d in range(1, n_cols):
        give_half(d).start()
    total = sent[half_span(c), :]
    for d in range(1, n_cols):
        give_half(d).wait_recv()
        total = total + halves[d - 1]
    acc[0] = total

    def add_up(s, k):
        at = 3 * s + k
        return remote(acc.at[s], into.at[at], sum_s.at[at], sum_r.at[at], sum_rounds[s][k])

    n_sums = len(sum_rounds)
    for s in range(n_sums):
        n_others = len(sum_rounds[s])
        for k in range(n_others):
            add_up(s, k).start()
        for k in range(n_others):
            add_up(s, k).wait_recv()
        total = acc[s] + into[3 * s]
        if n_others == 3:
            total = total + (into[3 * s + 1] + into[3 * s + 2])
        acc[s + 1] = total

    def hand_out(d):
        return remote(acc.at[n_sums], full.at[half_span(c)], full_s.at[d - 1], full_r.at[d - 1], siblings[d - 1])

    def hand_in(d):
        return remote(acc.at[n_sums], full.at[half_span(lax.rem(c + n_cols - d, n_cols))],
                      full_s.at[d - 1], full_r.at[d - 1], siblings[d - 1])

    for d in range(1, n_cols):
        hand_out(d).start()

    all_sent(near_s, (partner, c))

    @pl.when(can_fwd)
    def _():
        all_sent(far_s, (fwd_to, c))

    for d in range(1, n_cols):
        all_sent(sib_s.at[d - 1], siblings[d - 1])

        @pl.when(has_far)
        def _(d=d):
            all_sent(sib_s.at[n_cols - 1 + d - 1], siblings[d - 1])

        give_half(d).wait_send()
        for i in range(pieces):
            give(i, d).wait_send()
    for s in range(n_sums):
        for k in range(len(sum_rounds[s])):
            add_up(s, k).wait_send()
    for i in range(pieces):
        keep(i).wait()
    full[half_span(c), :] = acc[n_sums]
    for d in range(1, n_cols):
        hand_in(d).wait_recv()
        hand_out(d).wait_send()
    gram_out[...] = unpack(full[...], width)


def rows_and_gram(tile_cols, live_counts, block_vector, op_tiles, n_rows, n_cols):
    rows, width = block_vector.shape
    blocks, slots, tile, _ = op_tiles.shape
    part = rows // n_cols
    chunks = min(32, blocks)
    while part // chunks > tile:
        chunks *= 2
    pieces = 4
    sums = len(rounds_of(n_rows))
    others = max(1, n_cols - 1)
    packed = packed_rows(width, n_cols)
    half = packed // n_cols
    dma = pltpu.SemaphoreType.DMA
    vmem = pl.BlockSpec(memory_space=pltpu.VMEM)
    small = pl.BlockSpec(memory_space=pltpu.HBM)
    hbm = pl.BlockSpec(memory_space=pl.ANY)
    return pl.pallas_call(
        functools.partial(step_kernel, n_rows, n_cols, chunks, 8, 2, pieces),
        out_shape=(
            jax.ShapeDtypeStruct((part // tile, tile, width), F32),
            jax.ShapeDtypeStruct((width, width), F32),
        ),
        in_specs=[small, small, hbm, hbm],
        out_specs=(hbm, vmem),
        scratch_shapes=[
            pltpu.SMEM((slots, blocks), jnp.int32),
            pltpu.SMEM((blocks,), jnp.int32),
            pltpu.VMEM((blocks + 1, tile, 2 * width), BF16),
            pltpu.VMEM((2 * blocks, tile, width), F32),
            pltpu.VMEM((2 * blocks + 1, tile, 2 * width), BF16),
            pltpu.VMEM((2, blocks // chunks, slots, tile, tile), F32),
            pltpu.VMEM((blocks, 2 * tile, slots * tile), BF16),
            pltpu.VMEM((blocks, tile, width), F32),
            pltpu.VMEM((others, part // tile, tile, width), F32),
            pltpu.VMEM((width, 2 * width), F32),
            pltpu.VMEM((packed, width), F32),
            pltpu.VMEM((others, half, width), F32),
            pltpu.VMEM((sums + 1, half, width), F32),
            pltpu.VMEM((3 * sums, half, width), F32),
            pltpu.VMEM((packed, width), F32),
            dma((2,)), dma, dma((2,)), dma((pieces,)),
            dma, dma((chunks,)), dma, dma((chunks,)), dma((2 * others,)), dma((2 * others * chunks,)),
            dma((others * pieces,)), dma((others * pieces,)),
            dma((others,)), dma((others,)), dma((3 * sums,)), dma((3 * sums,)), dma((others,)), dma((others,)),
        ],
        compiler_params=pltpu.CompilerParams(collective_id=0, has_side_effects=True, vmem_limit_bytes=48 * MIB),
        name="rows_and_gram",
    )(tile_cols.T, live_counts, block_vector.reshape(blocks, tile, width), op_tiles)


def spread(x):
    x1 = x.astype(BF16).astype(F32)
    x2 = (x - x1).astype(BF16).astype(F32)
    return x1, x2, x - x1 - x2


def factor(gram):
    n = gram.shape[0]
    nb = PANEL
    lane = lax.broadcasted_iota(jnp.int32, (nb, n), 1)
    sub = lax.broadcasted_iota(jnp.int32, (nb, n), 0)
    eye = (lax.broadcasted_iota(jnp.int32, (n, n), 0) == lax.broadcasted_iota(jnp.int32, (n, n), 1)).astype(F32)
    left, right = gram, eye
    upper, inverse = [], []
    for p in range(n // nb):
        a = left[:nb]
        w = right[:nb]
        cols = [jnp.broadcast_to(a[:, p * nb + k:p * nb + k + 1], (nb, n)) for k in range(nb)]
        for j in range(nb):
            scale = lax.rsqrt(jnp.broadcast_to(cols[j][j:j + 1], (nb, n)))
            col = cols[j] * scale
            below = jnp.where(sub > j, col, 0.0)
            for k in range(j + 1, nb):
                cols[k] = cols[k] - below * jnp.broadcast_to(col[k:k + 1], (nb, n))
            a_row = jnp.broadcast_to(a[j:j + 1], (nb, n)) * scale
            w_row = jnp.broadcast_to(w[j:j + 1], (nb, n)) * scale
            a = jnp.where(sub == j, a_row, a - below * a_row)
            w = jnp.where(sub == j, w_row, w - below * w_row)
        upper.append(jnp.where(lane >= sub + p * nb, a, 0.0))
        inverse.append(w)
        rest = n - (p + 1) * nb
        if rest:
            a1, a2, a3 = spread(a)
            w1, w2, w3 = spread(w)
            lhs = jnp.concatenate([a1, a1, a2, a1, a2, a3], axis=0).T[n - rest:].astype(BF16)
            rhs_a = jnp.concatenate([a1, a2, a1, a3, a2, a1], axis=0)
            rhs_w = jnp.concatenate([w1, w2, w1, w3, w2, w1], axis=0)
            rhs = jnp.concatenate([rhs_a, rhs_w], axis=1).astype(BF16)
            change = jnp.dot(lhs, rhs, preferred_element_type=F32)
            left = left[nb:] - change[:, :n]
            right = right[nb:] - change[:, n:]
    return jnp.concatenate(upper, axis=0), jnp.concatenate(inverse, axis=0)


def basis_kernel(root, gram, rows, basis, r_factor, solve):
    @pl.when(pl.program_id(0) == 0)
    def _():
        upper, inverse = factor(gram[...])
        r_factor[...] = upper / root
        solve[...] = inverse * root

    width = rows.shape[1]
    x_hi, x_lo = split2(rows[...])
    s_hi, s_lo = split2(solve[...])
    both = lax.dot_general(x_hi, jnp.concatenate([s_hi, s_lo], axis=0), (((1,), (1,)), ((), ())),
                           preferred_element_type=F32)
    rest = lax.dot_general(x_lo, s_hi, (((1,), (1,)), ((), ())), preferred_element_type=F32)
    basis[...] = both[:, :width] + both[:, width:] + rest


def basis_of(gram, rows, root):
    part, width = rows.shape
    size = min(part, 1024)
    return pl.pallas_call(
        functools.partial(basis_kernel, root),
        out_shape=(jax.ShapeDtypeStruct((part, width), F32), jax.ShapeDtypeStruct((width, width), F32)),
        grid=(part // size,),
        in_specs=[
            pl.BlockSpec((width, width), lambda i: (0, 0)),
            pl.BlockSpec((size, width), lambda i: (i, 0)),
        ],
        out_specs=(
            pl.BlockSpec((size, width), lambda i: (i, 0)),
            pl.BlockSpec((width, width), lambda i: (0, 0)),
        ),
        scratch_shapes=[pltpu.VMEM((width, width), F32)],
        compiler_params=pltpu.CompilerParams(vmem_limit_bytes=24 * MIB),
        name="factor_and_basis",
    )(gram, rows)


def on_device(n_rows, n_cols, block_vector, op_tiles, tile_cols, live_counts):
    rows, gram = rows_and_gram(tile_cols, live_counts, block_vector, op_tiles, n_rows, n_cols)
    root = math.sqrt(block_vector.shape[0] * n_rows)
    return basis_of(gram, rows.reshape(-1, rows.shape[2]), root)


def solution(mesh):
    in_specs = (P("rows", None), P("rows", "cols", None, None), P("rows", "cols"), P("rows"))
    out_specs = (P(("rows", "cols"), None), P())
    return jax.shard_map(
        functools.partial(on_device, mesh.shape["rows"], mesh.shape["cols"]),
        mesh=mesh, in_specs=in_specs, out_specs=out_specs, check_vma=False,
    )
```

```python
import functools
import math

import jax
import jax.numpy as jnp
from jax import lax
from jax.experimental import pallas as pl
from jax.experimental.pallas import tpu as pltpu
from jax.sharding import PartitionSpec as P

MESH = pl.DeviceIdType.MESH
BF16 = jnp.bfloat16
F32 = jnp.float32
MIB = 1024 * 1024
PANEL = 16


def split2(x):
    hi = x.astype(BF16)
    lo = (x - hi.astype(F32)).astype(BF16)
    return hi, lo


def greet(peers):
    barrier = pltpu.get_barrier_semaphore()
    for cond, device in peers:
        if cond is None:
            pl.semaphore_signal(barrier, inc=1, device_id=device, device_id_type=MESH)
        else:
            @pl.when(cond)
            def _(device=device):
                pl.semaphore_signal(barrier, inc=1, device_id=device, device_id_type=MESH)
    total = 0
    for cond, _ in peers:
        total = total + (1 if cond is None else jnp.where(cond, 1, 0))
    pl.semaphore_wait(barrier, total)


def rounds_of(n_rows):
    rounds = []
    stride = 1
    while stride < n_rows:
        radix = min(4, n_rows // stride)
        rounds.append((stride, radix))
        stride *= radix
    return rounds


def packed_rows(width, n_cols):
    packed = width * 3 // 4
    return packed if width == 128 and packed % (8 * n_cols) == 0 else width


def pack(gram, rows):
    n = gram.shape[0]
    if rows == n:
        return gram
    h, q = n // 2, n // 4
    lane = lax.broadcasted_iota(jnp.int32, (q, n), 1)
    folded = jnp.where(lane < h, pltpu.roll(gram[h:h + q], h, axis=1), gram[h + q:])
    return jnp.concatenate([gram[:h], folded], axis=0)


def unpack(packed, n):
    if packed.shape[0] == n:
        return packed
    folded = packed[n // 2:]
    return jnp.concatenate([packed[:n // 2], pltpu.roll(folded, n // 2, axis=1), folded], axis=0)


def step_kernel(n_rows, n_cols, chunks, ahead, lag, pieces, cols_in, counts_in, own, tiles, rows_out, gram_out,
                cols, counts, own_split, halo, halo_split, stage, a_split, out, got, gram, sent, halves, acc, into, full,
                small_sem, own_sem, stage_sem, rows_sem, near_s, near_r, far_s, far_r, sib_s, sib_r, part_s, part_r,
                half_s, half_r, sum_s, sum_r, full_s, full_r):
    r = lax.axis_index("rows")
    c = lax.axis_index("cols")
    blocks, slots, tile, _ = tiles.shape
    rows, width = blocks * tile, own.shape[2]
    odd = lax.rem(r, 2)
    partner = r + 1 - 2 * odd
    fwd_to = r + 2 - 4 * odd
    far_from = r - 2 + 4 * odd
    can_fwd = (fwd_to >= 0) & (fwd_to < n_rows)
    has_far = (far_from >= 0) & (far_from < n_rows)
    part = rows // n_cols
    part_blocks = part // tile
    size = part // chunks
    near_slot = 1 - odd
    far_slot = odd
    siblings = [(r, lax.rem(c + d, n_cols)) for d in range(1, n_cols)]
    sum_rounds = []
    for first, radix in rounds_of(n_rows):
        digit = lax.rem(r // first, radix)
        low, high = lax.rem(digit, 2), digit // 2
        others = []
        for k in range(1, radix):
            new_low = 1 - low if k % 2 else low
            new_high = 1 - high if k // 2 else high
            others.append((r + (new_low - low + 2 * (new_high - high)) * first, c))
        sum_rounds.append(others)

    peers = [(None, (partner, c)), (can_fwd, (fwd_to, c)), (has_far, (far_from, c))]
    peers += [(None, device) for device in siblings]
    peers += [(None, device) for others in sum_rounds for device in others if device is not sum_rounds[0][0]]

    def remote(src, dst, send_sem, recv_sem, device):
        return pltpu.make_async_remote_copy(
            src_ref=src, dst_ref=dst, send_sem=send_sem, recv_sem=recv_sem, device_id=device, device_id_type=MESH)

    def chunk_place(i, col):
        row = col * part + i * size
        return row // tile, pl.ds(pl.multiple_of(lax.rem(row, tile), size), size)

    def own_at(i, col):
        block, span = chunk_place(i, col)
        return own.at[block, span]

    def halo_at(slot, i, col):
        block, span = chunk_place(i, col)
        return halo.at[slot * blocks + block, span]

    def near(i):
        return remote(own_at(i, c), halo_at(odd, i, c), near_s, near_r.at[i], (partner, c))

    def near_in(i):
        return remote(own_at(i, c), halo_at(near_slot, i, c), near_s, near_r.at[i], (partner, c))

    def far(i):
        return remote(halo_at(near_slot, i, c), halo_at(far_slot, i, c), far_s, far_r.at[i], (fwd_to, c))

    def sib(i, kind, d, incoming=False):
        slot = near_slot if kind == 0 else far_slot
        k = (kind * (n_cols - 1) + d - 1) * chunks + i
        col = lax.rem(c + n_cols - d, n_cols) if incoming else c
        return remote(halo_at(slot, i, c), halo_at(slot, i, col),
                      sib_s.at[kind * (n_cols - 1) + d - 1], sib_r.at[k], siblings[d - 1])

    def all_sent(sem, device):
        whole = halo.at[pl.ds(near_slot * blocks + c * part_blocks, part_blocks)]
        remote(whole, whole, sem, near_r.at[0], device).wait_send()

    group = 2 * (blocks // chunks)
    fetches = chunks // 2

    def fetch(i):
        k = lax.rem(i, 2)
        return pltpu.make_async_copy(tiles.at[pl.ds(i * group, group)], stage.at[k], stage_sem.at[k])

    bring_cols = pltpu.make_async_copy(cols_in, cols, small_sem.at[0])
    bring_counts = pltpu.make_async_copy(counts_in, counts, small_sem.at[1])
    bring_cols.start()
    bring_counts.start()
    bring_own = pltpu.make_async_copy(own, out, own_sem)
    bring_own.start()
    fetch(0).start()
    greet(peers)
    for i in range(ahead):
        near(i).start()

    def split_halo(slot, i, col):
        block, span = chunk_place(i, col)
        hi, lo = split2(halo[slot * blocks + block, span, :])
        halo_split[slot * blocks + block, span, :] = jnp.concatenate([hi, lo], axis=1)

    own_split[blocks] = jnp.zeros((tile, 2 * width), BF16)
    halo_split[2 * blocks] = jnp.zeros((tile, 2 * width), BF16)
    bring_cols.wait()
    bring_counts.wait()
    bring_own.wait()

    @pl.loop(0, blocks)
    def _(i):
        hi, lo = split2(out[i])
        own_split[i] = jnp.concatenate([hi, lo], axis=1)

    before = (r - 1) * blocks
    first_slot = c * slots

    def picked(row, ours):
        live = counts[row] - first_slot
        parts = []
        for s in range(slots):
            rel = cols[s, row] - before
            after_prev = (rel >= blocks).astype(jnp.int32)
            after_own = (rel >= 2 * blocks).astype(jnp.int32)
            mine = after_prev - after_own
            alive = (live > s).astype(jnp.int32)
            if ours:
                use = mine * alive
                at = use * (rel - blocks) + (1 - use) * blocks
                parts.append(own_split[lax.max(lax.min(at, blocks), 0)])
            else:
                use = (1 - mine) * alive
                at = use * (rel - blocks * after_own) + (1 - use) * (2 * blocks)
                parts.append(halo_split[lax.max(lax.min(at, 2 * blocks), 0)])
        return jnp.concatenate(parts, axis=0)

    def times(a, b):
        p = jnp.dot(a, b, preferred_element_type=F32)
        return (p[:tile, :width] + p[tile:, width:]) + (p[:tile, width:] + p[tile:, :width])

    def own_products(i):
        k = lax.rem(i, 2)
        fetch(i).wait()

        @pl.when(i + 1 < fetches)
        def _():
            fetch(i + 1).start()

        for j in range(group):
            row = i * group + j
            hi, lo = split2(jnp.concatenate([stage[k, j, s] for s in range(slots)], axis=1))
            a = jnp.concatenate([hi, lo], axis=0)
            a_split[row] = a
            out[row] = times(a, picked(row, True))

    @pl.loop(0, chunks + 2 * lag)
    def _(i):
        @pl.when(i < chunks)
        def _():
            near_in(i).wait_recv()

            @pl.when(can_fwd)
            def _():
                far(i).start()

            for d in range(1, n_cols):
                sib(i, 0, d).start()

            @pl.when(i + ahead < chunks)
            def _():
                near(i + ahead).start()

            split_halo(near_slot, i, c)

        @pl.when((i >= lag) & (i < chunks + lag) & has_far)
        def _():
            far(i - lag).wait_recv()
            for d in range(1, n_cols):
                sib(i - lag, 1, d).start()
            split_halo(far_slot, i - lag, c)

        @pl.when((i >= lag) & (i < chunks + lag))
        def _():
            for d in range(1, n_cols):
                sib(i - lag, 0, d, True).wait_recv()
                split_halo(near_slot, i - lag, lax.rem(c + n_cols - d, n_cols))

        @pl.when((i >= 2 * lag) & has_far)
        def _():
            for d in range(1, n_cols):
                sib(i - 2 * lag, 1, d, True).wait_recv()
                split_halo(far_slot, i - 2 * lag, lax.rem(c + n_cols - d, n_cols))

        @pl.when((i < chunks) & (lax.rem(i, 2) == 0))
        def _():
            own_products(i // 2)

    piece_blocks = part_blocks // pieces
    unroll = math.gcd(8, piece_blocks)

    def multiply_piece(col, i):
        first = col * part_blocks + i * piece_blocks

        @pl.loop(0, piece_blocks // unroll)
        def _(j):
            for u in range(unroll):
                row = first + j * unroll + u
                out[row] = out[row] + times(a_split[row], picked(row, False))

    def piece_span(col, i):
        return pl.ds(col * part_blocks + i * piece_blocks, piece_blocks)

    def give(i, d):
        k = (d - 1) * pieces + i
        return remote(out.at[piece_span(lax.rem(c + d, n_cols), i)], got.at[d - 1, piece_span(0, i)],
                      part_s.at[k], part_r.at[k], siblings[d - 1])

    def keep(i):
        return pltpu.make_async_copy(out.at[piece_span(c, i)], rows_out.at[piece_span(0, i)], rows_sem.at[i])

    for d in range(1, n_cols):
        @pl.loop(0, pieces)
        def _(i, d=d):
            multiply_piece(lax.rem(c + d, n_cols), i)
            give(i, d).start()

    gram[...] = jnp.zeros_like(gram)

    @pl.loop(0, pieces)
    def _(i):
        multiply_piece(c, i)
        x = out[piece_span(c, i)]
        for d in range(1, n_cols):
            give(i, d).wait_recv()
            x = x + got[d - 1, piece_span(0, i)]
        out[piece_span(c, i)] = x
        keep(i).start()
        hi, lo = split2(x.reshape(piece_blocks * tile, width))
        gram[...] += lax.dot_general(hi, jnp.concatenate([hi, lo], axis=1), (((0,), (0,)), ((), ())),
                                     preferred_element_type=F32)

    cross = gram[:, width:]
    sent[...] = pack(gram[:, :width] + (cross + cross.T), sent.shape[0])

    half = sent.shape[0] // n_cols

    def half_span(col):
        return pl.ds(pl.multiple_of(col * half, half), half)

    def give_half(d):
        return remote(sent.at[half_span(lax.rem(c + d, n_cols))], halves.at[d - 1],
                      half_s.at[d - 1], half_r.at[d - 1], siblings[d - 1])

    for d in range(1, n_cols):
        give_half(d).start()
    total = sent[half_span(c), :]
    for d in range(1, n_cols):
        give_half(d).wait_recv()
        total = total + halves[d - 1]
    acc[0] = total

    def add_up(s, k):
        at = 3 * s + k
        return remote(acc.at[s], into.at[at], sum_s.at[at], sum_r.at[at], sum_rounds[s][k])

    n_sums = len(sum_rounds)
    for s in range(n_sums):
        n_others = len(sum_rounds[s])
        for k in range(n_others):
            add_up(s, k).start()
        for k in range(n_others):
            add_up(s, k).wait_recv()
        total = acc[s] + into[3 * s]
        if n_others == 3:
            total = total + (into[3 * s + 1] + into[3 * s + 2])
        acc[s + 1] = total

    def hand_out(d):
        return remote(acc.at[n_sums], full.at[half_span(c)], full_s.at[d - 1], full_r.at[d - 1], siblings[d - 1])

    def hand_in(d):
        return remote(acc.at[n_sums], full.at[half_span(lax.rem(c + n_cols - d, n_cols))],
                      full_s.at[d - 1], full_r.at[d - 1], siblings[d - 1])

    for d in range(1, n_cols):
        hand_out(d).start()

    all_sent(near_s, (partner, c))

    @pl.when(can_fwd)
    def _():
        all_sent(far_s, (fwd_to, c))

    for d in range(1, n_cols):
        all_sent(sib_s.at[d - 1], siblings[d - 1])

        @pl.when(has_far)
        def _(d=d):
            all_sent(sib_s.at[n_cols - 1 + d - 1], siblings[d - 1])

        give_half(d).wait_send()
        for i in range(pieces):
            give(i, d).wait_send()
    for s in range(n_sums):
        for k in range(len(sum_rounds[s])):
            add_up(s, k).wait_send()
    for i in range(pieces):
        keep(i).wait()
    full[half_span(c), :] = acc[n_sums]
    for d in range(1, n_cols):
        hand_in(d).wait_recv()
        hand_out(d).wait_send()
    gram_out[...] = unpack(full[...], width)


def rows_and_gram(tile_cols, live_counts, block_vector, op_tiles, n_rows, n_cols):
    rows, width = block_vector.shape
    blocks, slots, tile, _ = op_tiles.shape
    part = rows // n_cols
    chunks = min(32, blocks)
    while part // chunks > tile:
        chunks *= 2
    pieces = 4
    sums = len(rounds_of(n_rows))
    others = max(1, n_cols - 1)
    packed = packed_rows(width, n_cols)
    half = packed // n_cols
    dma = pltpu.SemaphoreType.DMA
    vmem = pl.BlockSpec(memory_space=pltpu.VMEM)
    small = pl.BlockSpec(memory_space=pltpu.HBM)
    hbm = pl.BlockSpec(memory_space=pl.ANY)
    return pl.pallas_call(
        functools.partial(step_kernel, n_rows, n_cols, chunks, 8, 2, pieces),
        out_shape=(
            jax.ShapeDtypeStruct((part // tile, tile, width), F32),
            jax.ShapeDtypeStruct((width, width), F32),
        ),
        in_specs=[small, small, hbm, hbm],
        out_specs=(hbm, vmem),
        scratch_shapes=[
            pltpu.SMEM((slots, blocks), jnp.int32),
            pltpu.SMEM((blocks,), jnp.int32),
            pltpu.VMEM((blocks + 1, tile, 2 * width), BF16),
            pltpu.VMEM((2 * blocks, tile, width), F32),
            pltpu.VMEM((2 * blocks + 1, tile, 2 * width), BF16),
            pltpu.VMEM((2, 2 * (blocks // chunks), slots, tile, tile), F32),
            pltpu.VMEM((blocks, 2 * tile, slots * tile), BF16),
            pltpu.VMEM((blocks, tile, width), F32),
            pltpu.VMEM((others, part // tile, tile, width), F32),
            pltpu.VMEM((width, 2 * width), F32),
            pltpu.VMEM((packed, width), F32),
            pltpu.VMEM((others, half, width), F32),
            pltpu.VMEM((sums + 1, half, width), F32),
            pltpu.VMEM((3 * sums, half, width), F32),
            pltpu.VMEM((packed, width), F32),
            dma((2,)), dma, dma((2,)), dma((pieces,)),
            dma, dma((chunks,)), dma, dma((chunks,)), dma((2 * others,)), dma((2 * others * chunks,)),
            dma((others * pieces,)), dma((others * pieces,)),
            dma((others,)), dma((others,)), dma((3 * sums,)), dma((3 * sums,)), dma((others,)), dma((others,)),
        ],
        compiler_params=pltpu.CompilerParams(collective_id=0, has_side_effects=True, vmem_limit_bytes=48 * MIB),
        name="rows_and_gram",
    )(tile_cols.T, live_counts, block_vector.reshape(blocks, tile, width), op_tiles)


def spread(x):
    x1 = x.astype(BF16).astype(F32)
    x2 = (x - x1).astype(BF16).astype(F32)
    return x1, x2, x - x1 - x2


def factor(gram):
    n = gram.shape[0]
    nb = PANEL
    lane = lax.broadcasted_iota(jnp.int32, (nb, n), 1)
    sub = lax.broadcasted_iota(jnp.int32, (nb, n), 0)
    eye = (lax.broadcasted_iota(jnp.int32, (n, n), 0) == lax.broadcasted_iota(jnp.int32, (n, n), 1)).astype(F32)
    left, right = gram, eye
    upper, inverse = [], []
    for p in range(n // nb):
        a = left[:nb]
        w = right[:nb]
        cols = [jnp.broadcast_to(a[:, p * nb + k:p * nb + k + 1], (nb, n)) for k in range(nb)]
        for j in range(nb):
            scale = lax.rsqrt(jnp.broadcast_to(cols[j][j:j + 1], (nb, n)))
            col = cols[j] * scale
            below = jnp.where(sub > j, col, 0.0)
            for k in range(j + 1, nb):
                cols[k] = cols[k] - below * jnp.broadcast_to(col[k:k + 1], (nb, n))
            a_row = jnp.broadcast_to(a[j:j + 1], (nb, n)) * scale
            w_row = jnp.broadcast_to(w[j:j + 1], (nb, n)) * scale
            a = jnp.where(sub == j, a_row, a - below * a_row)
            w = jnp.where(sub == j, w_row, w - below * w_row)
        upper.append(jnp.where(lane >= sub + p * nb, a, 0.0))
        inverse.append(w)
        rest = n - (p + 1) * nb
        if rest:
            a1, a2, a3 = spread(a)
            w1, w2, w3 = spread(w)
            lhs = jnp.concatenate([a1, a1, a2, a1, a2, a3], axis=0).T[n - rest:].astype(BF16)
            rhs_a = jnp.concatenate([a1, a2, a1, a3, a2, a1], axis=0)
            rhs_w = jnp.concatenate([w1, w2, w1, w3, w2, w1], axis=0)
            rhs = jnp.concatenate([rhs_a, rhs_w], axis=1).astype(BF16)
            change = jnp.dot(lhs, rhs, preferred_element_type=F32)
            left = left[nb:] - change[:, :n]
            right = right[nb:] - change[:, n:]
    return jnp.concatenate(upper, axis=0), jnp.concatenate(inverse, axis=0)


def basis_kernel(root, gram, rows, basis, r_factor, solve):
    @pl.when(pl.program_id(0) == 0)
    def _():
        upper, inverse = factor(gram[...])
        r_factor[...] = upper / root
        solve[...] = inverse * root

    width = rows.shape[1]
    x_hi, x_lo = split2(rows[...])
    s_hi, s_lo = split2(solve[...])
    both = lax.dot_general(x_hi, jnp.concatenate([s_hi, s_lo], axis=0), (((1,), (1,)), ((), ())),
                           preferred_element_type=F32)
    rest = lax.dot_general(x_lo, s_hi, (((1,), (1,)), ((), ())), preferred_element_type=F32)
    basis[...] = both[:, :width] + both[:, width:] + rest


def basis_of(gram, rows, root):
    part, width = rows.shape
    size = min(part, 1024)
    return pl.pallas_call(
        functools.partial(basis_kernel, root),
        out_shape=(jax.ShapeDtypeStruct((part, width), F32), jax.ShapeDtypeStruct((width, width), F32)),
        grid=(part // size,),
        in_specs=[
            pl.BlockSpec((width, width), lambda i: (0, 0)),
            pl.BlockSpec((size, width), lambda i: (i, 0)),
        ],
        out_specs=(
            pl.BlockSpec((size, width), lambda i: (i, 0)),
            pl.BlockSpec((width, width), lambda i: (0, 0)),
        ),
        scratch_shapes=[pltpu.VMEM((width, width), F32)],
        compiler_params=pltpu.CompilerParams(vmem_limit_bytes=24 * MIB),
        name="factor_and_basis",
    )(gram, rows)


def on_device(n_rows, n_cols, block_vector, op_tiles, tile_cols, live_counts):
    rows, gram = rows_and_gram(tile_cols, live_counts, block_vector, op_tiles, n_rows, n_cols)
    root = math.sqrt(block_vector.shape[0] * n_rows)
    return basis_of(gram, rows.reshape(-1, rows.shape[2]), root)


def solution(mesh):
    in_specs = (P("rows", None), P("rows", "cols", None, None), P("rows", "cols"), P("rows"))
    out_specs = (P(("rows", "cols"), None), P())
    return jax.shard_map(
        functools.partial(on_device, mesh.shape["rows"], mesh.shape["cols"]),
        mesh=mesh, in_specs=in_specs, out_specs=out_specs, check_vma=False,
    )
```
